128 devices in a mesh: wide: 16 (over x, y_lo, core), narrow: 8 (over y_hi, z).
Axes of the slice: x: 4, y: 4 (y_hi: 2, y_lo: 2; y = y_hi * 2 + y_lo), z: 4, core: 2. Of those that a mesh axis runs over, the one named last changes fastest.
Arguments:
- picture_embedding_matrix: bfloat16 [131072, 1152], P(('wide', 'narrow')), may hold values from -0.19921875 to 0.19921875
- caption_embedding_matrix: bfloat16 [131072, 1152], P(('wide', 'narrow')), may hold values from -0.19921875 to 0.19921875
- inverse_softness: float32 [1], replicated, may hold values from 3 to 16
- additive_shift_term: float32 [1], replicated, may hold values from -3 to 0
Outputs:
- image_grad: float32 [131072, 1152], P(('wide', 'narrow'))
- text_grad: float32 [131072, 1152], P(('wide', 'narrow'))
The draws below stay inside these ranges and needn't reach their ends.
All inputs are finite; a program needn't handle non-finite values.
Results may differ from the reference program's by a relative error of at most 0.0046.
Values may be sent and summed in bfloat16 or wider, within the bound.
No kernel may reach another device: no remote copies, remote signals or barrier semaphores. Data moves between devices by JAX's collectives and lax.ppermute only.
A program may use at most 128 MiB of HBM per device.

```python
import math
import jax
import jax.numpy as jnp
from jax import lax

D = 1152
PAIRS_PER_SHARD = 1024
BAND = 4
PAIRS = 131072
N_WIDE = 16
N_NARROW = 8


def level_of(own_key, shape, pieces, low, largest):
    gain = 1.0
    for dim, shards_of in pieces:
        heights = jax.random.uniform(jax.random.fold_in(jax.random.fold_in(own_key, 6), dim), (shards_of,), jnp.float32, low / len(pieces), largest / len(pieces))
        gain = gain * jnp.repeat(jnp.exp(heights), shape[dim] // shards_of).reshape((-1,) + (1,) * (len(shape) - 1 - dim))
    return gain


def centred(own_key, dims, scale, most, cuts=(), kind=jnp.bfloat16):
    values = scale * jax.random.normal(own_key, dims, jnp.float32)
    if cuts:
        values = values * level_of(own_key, dims, cuts, -0.22, 0.18)
    return jnp.clip(values, -most, most).astype(kind)


def setup_inputs(seed: int = 0) -> dict:
    key_of = jax.random.split(jax.random.key(seed), 5)
    return {
        "picture_embedding_matrix": centred(key_of[0], (PAIRS, D), 0.03, 0.19921875, ((0, 128),)),
        "caption_embedding_matrix": centred(key_of[1], (PAIRS, D), 0.03, 0.19921875, ((0, 128),)),
        "inverse_softness": jnp.clip(jnp.exp(jax.random.uniform(key_of[2], (1,), jnp.float32, math.log(3.0), math.log(16.0))), 3.0, 16.0),
        "additive_shift_term": jnp.clip(jax.random.uniform(key_of[3], (1,), jnp.float32, -3.0, 0.0), -3.0, 0.0),
    }


def rescale_lines_to_length_one(raw):
    widened_float32 = raw.astype(jnp.float32)
    inverse = lax.rsqrt(lax.optimization_barrier(jnp.sum(widened_float32 * widened_float32, axis=-1, keepdims=True)) + 1e-06)
    return (widened_float32 * inverse, inverse)

def pair_weights(logits, positive):
    signs = 2.0 * positive - 1.0
    return (-signs * jax.nn.sigmoid(-signs * logits)).astype(jnp.bfloat16)

def back_normal(unit, inverse, direction):
    inner = lax.optimization_barrier(jnp.sum(unit * direction, axis=-1, keepdims=True))
    return inverse * (direction - unit * inner)

def reference(picture_embedding_matrix, caption_embedding_matrix, inverse_softness, additive_shift_term):
    tile_count = N_WIDE * N_NARROW
    image_unit, image_inv = rescale_lines_to_length_one(picture_embedding_matrix)
    text_unit, text_inv = rescale_lines_to_length_one(caption_embedding_matrix)
    image_low = image_unit.astype(jnp.bfloat16).reshape(tile_count, PAIRS_PER_SHARD, D)
    text_low = text_unit.astype(jnp.bfloat16).reshape(tile_count, PAIRS_PER_SHARD, D)
    similarity_multiplier = inverse_softness[0]
    bias_value = additive_shift_term[0]
    rows_idx = jnp.arange(PAIRS_PER_SHARD, dtype=jnp.int32)
    diagonal = (rows_idx[:, None] == rows_idx[None, :]).astype(jnp.float32)
    image_dir = jnp.zeros((tile_count, PAIRS_PER_SHARD, D), jnp.float32)
    text_dir = jnp.zeros((tile_count, PAIRS_PER_SHARD, D), jnp.float32)
    for offset in range(BAND):
        moved = jnp.roll(text_low, offset, axis=0)
        positive = diagonal if offset == 0 else jnp.zeros_like(diagonal)

        def one_block(pair):
            left, right = pair
            logits = similarity_multiplier * jnp.dot(left, right.T, preferred_element_type=jnp.float32) + bias_value
            pair_label_weights = pair_weights(logits, positive)
            to_image = similarity_multiplier * jnp.dot(pair_label_weights, right, preferred_element_type=jnp.float32)
            to_text = similarity_multiplier * jnp.dot(pair_label_weights.T, left, preferred_element_type=jnp.float32)
            return (to_image, to_text)
        to_image, to_text = lax.map(one_block, (image_low, moved))
        image_dir = image_dir + to_image
        text_dir = text_dir + jnp.roll(to_text, -offset, axis=0)
    image_grad = back_normal(image_unit, image_inv, image_dir.reshape(PAIRS, D))
    text_grad = back_normal(text_unit, text_inv, text_dir.reshape(PAIRS, D))
    return (image_grad, text_grad)
```

```python
import functools

import jax
import jax.numpy as jnp
from jax import lax
from jax.experimental import pallas as pl
from jax.experimental.pallas import tpu as pltpu
from jax.sharding import PartitionSpec as P

AXES = ("wide", "narrow")
RING = 4
VMEM_BYTES = 48 * 1024 * 1024


def ring_route(step, count):
    return [(d, d - d % RING + (d + step) % RING) for d in range(count)]


def line_route(step, count):
    return [(d, (d + step) % count) for d in range(count)]


def send(block, route):
    return lax.ppermute(block, AXES, route)


def unit_rows(raw):
    wide = raw.astype(jnp.float32)
    inverse = lax.rsqrt(jnp.sum(wide * wide, axis=-1, keepdims=True) + 1e-06)
    return wide * inverse, inverse


def unit_kernel(raw_ref, *refs):
    unit, _ = unit_rows(raw_ref[...])
    refs[-1][0] = unit.astype(jnp.bfloat16)


def unit_images(raw, slot, held=None):
    rows, width = raw.shape
    tile = rows // 4
    aliased = [] if held is None else [held]
    return pl.pallas_call(
        unit_kernel,
        grid=(4,),
        out_shape=jax.ShapeDtypeStruct((2, rows, width), jnp.bfloat16),
        in_specs=[pl.BlockSpec((tile, width), lambda i: (i, 0))]
        + [pl.BlockSpec(memory_space=pl.ANY)] * len(aliased),
        out_specs=pl.BlockSpec((1, tile, width), lambda i: (slot, i, 0)),
        input_output_aliases={} if held is None else {1: 0},
        cost_estimate=pl.CostEstimate(
            flops=4 * rows * width, bytes_accessed=4 * rows * width, transcendentals=0
        ),
    )(raw, *aliased)


def dot(left, right, contract):
    return lax.dot_general(
        left, right, (contract, ((), ())), preferred_element_type=jnp.float32
    )


def pair_kernel(own, tile, slot_ref, scalars_ref, text_ref, images_ref, *refs):
    if own:
        sum_in = None
        partial_ref, sum_ref, images, low, weights, total, sems = refs
    else:
        sum_in, partial_ref, sum_ref, images, low, weights, total, sems = refs
    rows = text_ref.shape[0]
    slot = slot_ref[0]
    scale = scalars_ref[0]
    bias = scalars_ref[1]
    load_images = pltpu.make_async_copy(images_ref.at[slot], images, sems.at[0])
    load_images.start()
    if own:
        zero_tile = total.at[pl.ds(0, tile)]
        total[pl.ds(0, tile), :] = jnp.zeros((tile, total.shape[1]), jnp.float32)
        clears = [
            pltpu.make_async_copy(
                zero_tile, sum_ref.at[1, pl.ds(i * tile, tile)], sems.at[1 + i]
            )
            for i in range(total.shape[0] // tile)
        ]
        for clear in clears:
            clear.start()
    else:
        load_sum = pltpu.make_async_copy(sum_in.at[slot], total, sems.at[1])
        load_sum.start()
    unit, _ = unit_rows(text_ref[...])
    low[...] = unit.astype(jnp.bfloat16)
    load_images.wait()

    @pl.loop(0, rows // tile)
    def _(i):
        here = pl.ds(pl.multiple_of(i * tile, tile), tile)
        logits = scale * dot(low[here, :], images[...], ((1,), (1,))) + bias
        if own:
            row = i * tile + lax.broadcasted_iota(jnp.int32, logits.shape, 0)
            column = lax.broadcasted_iota(jnp.int32, logits.shape, 1)
            sign = jnp.where(row == column, -1.0, 1.0)
            weight = sign / (1.0 + jnp.exp(-(sign * logits)))
        else:
            weight = 1.0 / (1.0 + jnp.exp(-logits))
        weights[here, :] = weight.astype(jnp.bfloat16)
        product = dot(weights[here, :], images[...], ((1,), (0,)))
        partial_ref[here, :] = (scale * product).astype(partial_ref.dtype)

    if own:
        for clear in clears:
            clear.wait()
    else:
        load_sum.wait()

    @pl.loop(0, total.shape[0] // tile)
    def _(i):
        here = pl.ds(pl.multiple_of(i * tile, tile), tile)
        product = scale * dot(weights[:, here], low[...], ((0,), (0,)))
        total[here, :] = product if own else total[here, :] + product

    store_sum = pltpu.make_async_copy(total, sum_ref.at[slot], sems.at[0])
    store_sum.start()
    store_sum.wait()


def pair(slot, scalars, text, images, sums, partial_dtype, tile=256):
    own = sums is None
    rows, width = text.shape
    image_rows = images.shape[1]
    any_spec = pl.BlockSpec(memory_space=pl.ANY)
    smem = pl.BlockSpec(memory_space=pltpu.SMEM)
    vmem = pl.BlockSpec(memory_space=pltpu.VMEM)
    return pl.pallas_call(
        functools.partial(pair_kernel, own, tile),
        out_shape=(
            jax.ShapeDtypeStruct((rows, width), partial_dtype),
            jax.ShapeDtypeStruct((2, image_rows, width), jnp.float32),
        ),
        in_specs=[smem, smem, vmem, any_spec] + ([] if own else [any_spec]),
        out_specs=(vmem, any_spec),
        input_output_aliases={} if own else {4: 1},
        scratch_shapes=[
            pltpu.VMEM((image_rows, width), jnp.bfloat16),
            pltpu.VMEM((rows, width), jnp.bfloat16),
            pltpu.VMEM((rows, image_rows), jnp.bfloat16),
            pltpu.VMEM((image_rows, width), jnp.float32),
            pltpu.SemaphoreType.DMA((1 + image_rows // tile,)),
        ],
        compiler_params=pltpu.CompilerParams(vmem_limit_bytes=VMEM_BYTES),
        cost_estimate=pl.CostEstimate(
            flops=6 * rows * image_rows * width,
            bytes_accessed=8 * image_rows * width + 4 * rows * width,
            transcendentals=rows * image_rows,
        ),
    )(slot, scalars, text, images, *([] if own else [sums]))


def finish_kernel(raw_ref, base_ref, *refs):
    grad_ref = refs[-1]
    unit, inverse = unit_rows(raw_ref[...])
    direction = base_ref[...].reshape(unit.shape)
    for part in refs[:-1]:
        direction = direction + part[...].astype(jnp.float32)
    inner = jnp.sum(unit * direction, axis=-1, keepdims=True)
    grad_ref[...] = inverse * (direction - unit * inner)


def finish(raw, base, parts, tile=128):
    rows, width = raw.shape
    flat = pl.BlockSpec((tile, width), lambda i: (i, 0))
    base_spec = flat if base.ndim == 2 else pl.BlockSpec((1, tile, width), lambda i: (0, i, 0))
    return pl.pallas_call(
        finish_kernel,
        grid=(rows // tile,),
        out_shape=jax.ShapeDtypeStruct((rows, width), jnp.float32),
        in_specs=[flat, base_spec] + [flat] * len(parts),
        out_specs=flat,
        cost_estimate=pl.CostEstimate(
            flops=8 * rows * width, bytes_accessed=12 * rows * width, transcendentals=0
        ),
    )(raw, base, *parts)


def body(images_raw, texts_raw, inverse_softness, additive_shift_term):
    count = lax.axis_size("wide") * lax.axis_size("narrow")
    z = lax.axis_index("narrow") % RING
    scalars = jnp.concatenate([inverse_softness, additive_shift_term])
    slots = [jnp.zeros((1,), jnp.int32)] + [
        jnp.where(z < RING - t, 1, 0).astype(jnp.int32).reshape(1) for t in (1, 2, 3)
    ]
    up, down = ring_route(1, count), ring_route(-1, count)
    half = texts_raw.shape[0] // 2
    own_a, own_b = texts_raw[:half], texts_raw[half:]

    images_next_raw = send(images_raw, line_route(-RING, count))
    left_a = send(own_a, up)
    right_b = send(own_b, down)

    images = unit_images(images_raw, 0)
    text_own, sums = pair(slots[0], scalars, texts_raw, images, None, jnp.float32)

    left_b = send(own_b, up)
    right_a = send(own_a, down)
    far_a = send(left_a, up)
    far_b = send(right_b, down)

    images = unit_images(images_next_raw, 1, images)
    step = lambda t, text, total, kind: pair(slots[t], scalars, text, images, total, kind)
    part_left_a, sums = step(3, left_a, sums, jnp.bfloat16)
    part_right_b, sums = step(1, right_b, sums, jnp.bfloat16)
    from_right_a = send(part_left_a, down)
    from_left_b = send(part_right_b, up)
    part_far_a, sums = step(2, far_a, sums, jnp.bfloat16)
    part_far_b, sums = step(2, far_b, sums, jnp.bfloat16)
    far_for_right_a = send(part_far_a, up)
    far_for_left_b = send(part_far_b, down)
    part_right_a, sums = step(1, right_a, sums, jnp.float32)
    part_left_b, sums = step(3, left_b, sums, jnp.float32)
    images_back = send(sums[1].astype(jnp.bfloat16), line_route(RING, count))
    from_left_a = send(
        (part_right_a + far_for_right_a.astype(jnp.float32)).astype(jnp.bfloat16), up
    )
    from_right_b = send(
        (part_left_b + far_for_left_b.astype(jnp.float32)).astype(jnp.bfloat16), down
    )
    image_grad = finish(images_raw, sums, [images_back])
    text_grad = finish(
        texts_raw,
        text_own,
        [
            jnp.concatenate([from_right_a, from_left_b]),
            jnp.concatenate([from_left_a, from_right_b]),
        ],
    )
    return image_grad, text_grad


def solution(mesh):
    spec = P(AXES, None)
    return jax.shard_map(
        body,
        mesh=mesh,
        in_specs=(spec, spec, P(), P()),
        out_specs=(spec, spec),
        check_vma=False,
    )
```

```python
import functools

import jax
import jax.numpy as jnp
from jax import lax
from jax.experimental import pallas as pl
from jax.experimental.pallas import tpu as pltpu
from jax.sharding import PartitionSpec as P

AXES = ("wide", "narrow")
RING = 4
LOG2_E = 1.4426950408889634
VMEM_BYTES = 14 * 1024 * 1024
COST = pl.CostEstimate(flops=1000, bytes_accessed=1000, transcendentals=0)
IN_SMEM = pl.BlockSpec(memory_space=pltpu.SMEM)
IN_VMEM = pl.BlockSpec(memory_space=pltpu.VMEM)


def ring_route(step, count):
    return [(d, d - d % RING + (d + step) % RING) for d in range(count)]


def line_route(step, count):
    return [(d, (d + step) % count) for d in range(count)]


def send(block, route):
    return lax.ppermute(block, AXES, route)


def params(limit=VMEM_BYTES):
    return pltpu.CompilerParams(vmem_limit_bytes=limit)


def dot(left, right, left_dim, right_dim):
    contract = (((left_dim,), (right_dim,)), ((), ()))
    return lax.dot_general(left, right, contract, preferred_element_type=jnp.float32)


def unit_rows(raw):
    wide = raw.astype(jnp.float32)
    inverse = lax.rsqrt(jnp.sum(wide * wide, axis=-1, keepdims=True) + 1e-06)
    return wide * inverse, inverse


def halves_kernel(texts_ref, first_ref, second_ref, sems):
    half = first_ref.shape[0]
    copies = [
        pltpu.make_async_copy(texts_ref.at[pl.ds(k * half, half)], out, sems.at[k])
        for k, out in enumerate((first_ref, second_ref))
    ]
    for copy in copies:
        copy.start()
    for copy in copies:
        copy.wait()


def halves(texts):
    rows, width = texts.shape
    return pl.pallas_call(
        halves_kernel,
        out_shape=[jax.ShapeDtypeStruct((rows // 2, width), texts.dtype)] * 2,
        in_specs=[pl.BlockSpec(memory_space=pl.ANY)],
        out_specs=[IN_VMEM] * 2,
        scratch_shapes=[pltpu.SemaphoreType.DMA((2,))],
        compiler_params=params(),
        cost_estimate=COST,
    )(texts)


def unit_kernel(raw_ref, *refs):
    unit, _ = unit_rows(raw_ref[...])
    refs[-1][0] = unit.astype(jnp.bfloat16)


def unit_images(raw, slot, held=None):
    rows, width = raw.shape
    tile = rows // 2
    aliased = [] if held is None else [held]
    return pl.pallas_call(
        unit_kernel,
        grid=(rows // tile,),
        out_shape=jax.ShapeDtypeStruct((2, rows, width), jnp.bfloat16),
        in_specs=[pl.BlockSpec((tile, width), lambda i: (i, 0))]
        + [pl.BlockSpec(memory_space=pl.ANY)] * len(aliased),
        out_specs=pl.BlockSpec((1, tile, width), lambda i: (slot, i, 0)),
        input_output_aliases={} if held is None else {1: 0},
        compiler_params=params(),
        cost_estimate=COST,
    )(raw, *aliased)


def pair_kernel(own, tile, texts_count, slots_ref, scalars_ref, images_ref, *refs):
    texts, pieces = refs[:texts_count], refs[texts_count:-2]
    weights_ref, low_ref = refs[-2:]
    scale, bias = scalars_ref[0], scalars_ref[1]
    rate, offset = -LOG2_E * scale, -LOG2_E * bias
    tiles = [
        (k, start) for k in range(texts_count) for start in range(0, texts[k].shape[0], tile)
    ]
    slots = [0 if own else slots_ref[k] for k in range(texts_count)]
    places = [(piece, start) for piece in pieces for start in range(0, piece.shape[0], tile)]

    def exponents(i):
        k, start = tiles[i]
        unit, _ = unit_rows(texts[k][start : start + tile, :])
        low = unit.astype(jnp.bfloat16)
        low_ref[i * tile : (i + 1) * tile, :] = low
        return rate * dot(low, images_ref[slots[k]], 1, 1) + offset

    ahead = exponents(0)
    for i, (k, _) in enumerate(tiles):
        exponent = ahead
        if i + 1 < len(tiles):
            ahead = exponents(i + 1)
        if own:
            row = i * tile + lax.broadcasted_iota(jnp.int32, exponent.shape, 0)
            column = lax.broadcasted_iota(jnp.int32, exponent.shape, 1)
            sign = jnp.where(row == column, -1.0, 1.0)
            weight = (sign / (1.0 + jnp.exp2(sign * exponent))).astype(jnp.bfloat16)
        else:
            weight = (1.0 / (1.0 + jnp.exp2(exponent))).astype(jnp.bfloat16)
        weights_ref[i * tile : (i + 1) * tile, :] = weight
        product = scale * dot(weight, images_ref[slots[k]], 1, 0)
        piece, start = places[i]
        piece[start : start + tile, :] = product.astype(piece.dtype)


def pair_sum_kernel(tile, slots_ref, scalars_ref, images_ref, weights_ref, low_ref, own_ref, *refs):
    texts, pieces = refs[:2], refs[2:4]
    total_ref, next_ref, weights, low, sums = refs[4:]
    pair_kernel(
        False, tile, 2, slots_ref, scalars_ref, images_ref, *texts, *pieces, weights, low
    )
    depth = low.shape[0] // 2
    scale = scalars_ref[0]

    @pl.loop(0, own_ref.shape[0] // tile)
    def _(i):
        here = pl.ds(pl.multiple_of(i * tile, tile), tile)
        sums[0] = own_ref[here, :]
        sums[1] = jnp.zeros(sums.shape[1:], jnp.float32)
        for k, (many, units) in enumerate([(weights, low)] * 2 + [(weights_ref, low_ref)] * 2):
            rows = slice(k % 2 * depth, (k % 2 + 1) * depth)
            sums[slots_ref[k]] += scale * dot(many[rows, here], units[rows, :], 0, 0)
        total_ref[here, :] = sums[0]
        next_ref[here, :] = sums[1]


def pair_sum(slots, scalars, images, texts, weights, low, own, tile=256):
    _, image_rows, width = images.shape
    half = texts[0].shape[0]
    direction = jax.ShapeDtypeStruct((image_rows, width), jnp.float32)
    return pl.pallas_call(
        functools.partial(pair_sum_kernel, tile),
        out_shape=[jax.ShapeDtypeStruct((half, width), jnp.bfloat16)] * 2 + [direction] * 2,
        in_specs=[IN_SMEM, IN_SMEM] + [IN_VMEM] * 6,
        out_specs=[IN_VMEM] * 4,
        scratch_shapes=[
            pltpu.VMEM((2 * half, image_rows), jnp.bfloat16),
            pltpu.VMEM((2 * half, width), jnp.bfloat16),
            pltpu.VMEM((2, tile, width), jnp.float32),
        ],
        compiler_params=params(),
        cost_estimate=COST,
    )(slots, scalars, images, weights, low, own, *texts)


def pair(slots, scalars, images, texts, pieces, partial_dtype, own=False, tile=256):
    _, image_rows, width = images.shape
    rows = sum(pieces)
    outs = [jax.ShapeDtypeStruct((piece, width), partial_dtype) for piece in pieces]
    outs += [
        jax.ShapeDtypeStruct((rows, image_rows), jnp.bfloat16),
        jax.ShapeDtypeStruct((rows, width), jnp.bfloat16),
    ]
    return pl.pallas_call(
        functools.partial(pair_kernel, own, tile, len(texts)),
        out_shape=outs,
        in_specs=[IN_SMEM, IN_SMEM, IN_VMEM] + [IN_VMEM] * len(texts),
        out_specs=[IN_VMEM] * len(outs),
        compiler_params=params(),
        cost_estimate=COST,
    )(slots, scalars, images, *texts)


def first_sum_kernel(tile, scalars_ref, weights_ref, low_ref, own_ref):
    for start in range(0, own_ref.shape[0], tile):
        here = slice(start, start + tile)
        own_ref[here, :] = scalars_ref[0] * dot(weights_ref[:, here], low_ref[...], 0, 0)


def first_sum(scalars, weights, low, tile=256):
    return pl.pallas_call(
        functools.partial(first_sum_kernel, tile),
        out_shape=jax.ShapeDtypeStruct((weights.shape[1], low.shape[1]), jnp.float32),
        in_specs=[IN_SMEM, IN_VMEM, IN_VMEM],
        out_specs=IN_VMEM,
        compiler_params=params(),
        cost_estimate=COST,
    )(scalars, weights, low)


def last_sum_kernel(tile, slots_ref, scalars_ref, own_ref, next_ref, weights_ref, low_ref, *refs):
    total_ref, ready_ref = refs
    next_share = scalars_ref[0] * slots_ref[0].astype(jnp.float32)
    own_share = scalars_ref[0] - next_share

    @pl.loop(0, own_ref.shape[0] // tile)
    def _(i):
        here = pl.ds(pl.multiple_of(i * tile, tile), tile)
        product = dot(weights_ref[:, here], low_ref[...], 0, 0)
        ready_ref[here, :] = (next_ref[here, :] + next_share * product).astype(ready_ref.dtype)
        total_ref[here, :] = own_ref[here, :] + own_share * product


def last_sum(slots, scalars, own, following, weights, low, tile=256):
    return pl.pallas_call(
        functools.partial(last_sum_kernel, tile),
        out_shape=[own, jax.ShapeDtypeStruct(own.shape, jnp.bfloat16)],
        in_specs=[IN_SMEM, IN_SMEM] + [IN_VMEM] * 4,
        out_specs=[IN_VMEM] * 2,
        compiler_params=params(),
        cost_estimate=COST,
    )(slots, scalars, own, following, weights, low)


def finish_rows(raw, direction):
    unit, inverse = unit_rows(raw)
    inner = jnp.sum(unit * direction, axis=-1, keepdims=True)
    return inverse * (direction - unit * inner)


def finish_images_kernel(raw_ref, own_ref, back_ref, grad_ref):
    direction = own_ref[...] + back_ref[...].astype(jnp.float32)
    grad_ref[...] = finish_rows(raw_ref[...], direction)


def finish_images(raw, own, back):
    rows, width = raw.shape
    tile = rows // 2
    flat = pl.BlockSpec((tile, width), lambda i: (i, 0))
    return pl.pallas_call(
        finish_images_kernel,
        grid=(rows // tile,),
        out_shape=jax.ShapeDtypeStruct((rows, width), jnp.float32),
        in_specs=[flat] * 3,
        out_specs=flat,
        compiler_params=params(),
        cost_estimate=COST,
    )(raw, own, back)


def finish_texts_kernel(phase, raw_ref, own_ref, *refs):
    halves_refs, quarter_refs, grad_ref = refs[:2], refs[2:4], refs[-1]
    rows = raw_ref.shape[0]
    for step in range(2):

        @pl.when(pl.program_id(0) == step)
        def _():
            near = halves_refs[step][phase * rows : (phase + 1) * rows, :]
            direction = own_ref[...] + near.astype(jnp.float32)
            direction = direction + quarter_refs[step][...].astype(jnp.float32)
            grad_ref[...] = finish_rows(raw_ref[...], direction)


def finish_texts(phase, raw, own, halves_in, quarters_in, held=None):
    rows, width = raw.shape
    flat = pl.BlockSpec((rows // 4, width), lambda i: (2 * i + phase, 0))
    aliased = [] if held is None else [held]
    return pl.pallas_call(
        functools.partial(finish_texts_kernel, phase),
        grid=(2,),
        out_shape=jax.ShapeDtypeStruct((rows, width), jnp.float32),
        in_specs=[flat] * 2
        + [IN_VMEM] * 4
        + [pl.BlockSpec(memory_space=pl.ANY)] * len(aliased),
        out_specs=flat,
        input_output_aliases={} if held is None else {6: 0},
        compiler_params=params(),
        cost_estimate=COST,
    )(raw, own, *halves_in, *quarters_in, *aliased)


def after(value, *earlier):
    return lax.optimization_barrier((value, *earlier))[0]


def body(images_raw, texts_raw, inverse_softness, additive_shift_term):
    count = lax.axis_size("wide") * lax.axis_size("narrow")
    z = lax.axis_index("narrow") % RING
    scalars = jnp.concatenate([inverse_softness, additive_shift_term])
    slot = [jnp.zeros((1,), jnp.int32)] + [
        jnp.where(z < RING - t, 1, 0).astype(jnp.int32).reshape(1) for t in (1, 2, 3)
    ]
    slots = lambda *places: jnp.concatenate([slot[t] for t in places])
    up, down = ring_route(1, count), ring_route(-1, count)
    rows = texts_raw.shape[0]
    half, quarter = rows // 2, rows // 4

    images_next_raw = send(images_raw, line_route(-RING, count))
    own_a, own_b = halves(texts_raw)
    left_a = send(own_a, up)
    right_b = send(own_b, down)
    images = unit_images(images_raw, 0)
    text_own, weights_0, low_0 = pair(
        slots(0), scalars, images, [texts_raw], [rows], jnp.float32, own=True
    )
    own_sum = first_sum(scalars, weights_0, low_0)
    left_b = send(after(own_b, own_sum), up)
    right_a = send(after(own_a, own_sum), down)
    far_a = send(after(left_a, own_sum), up)
    far_b = send(after(right_b, own_sum), down)

    images = unit_images(images_next_raw, 1, images)
    left_part_a, right_part_b, weights_x, low_x = pair(
        slots(3, 1), scalars, images, [left_a, right_b], [half] * 2, jnp.bfloat16
    )
    from_right_a = send(left_part_a, down)
    from_left_b = send(right_part_b, up)
    right_part_a, left_part_b, own_sum, next_sum = pair_sum(
        slots(1, 3, 3, 1), scalars, images, [right_a, left_b], weights_x, low_x, own_sum
    )
    *far_parts, weights_2, low_2 = pair(
        after(slots(2, 2), own_sum), scalars, images, [far_a, far_b], [quarter] * 4, jnp.bfloat16
    )
    own_sum, next_sum = last_sum(slots(2), scalars, own_sum, next_sum, weights_2, low_2)
    far_a1, far_b1 = send(far_parts[0], up), send(far_parts[2], down)
    images_back = send(next_sum, line_route(RING, count))
    far_a2, far_b2 = (
        send(after(far_parts[1], next_sum, from_right_a, from_left_b), up),
        send(after(far_parts[3], next_sum, from_right_a, from_left_b), down),
    )

    def relay(part, far, route, *earlier):
        total = after(part, own_sum, *earlier).astype(jnp.float32) + far.astype(jnp.float32)
        return send(total.astype(jnp.bfloat16), route)

    near = (from_right_a, from_left_b)
    from_left_a1 = relay(right_part_a[:quarter], far_a1, up, *near)
    from_right_b1 = relay(left_part_b[:quarter], far_b1, down, *near)
    from_left_a2 = relay(right_part_a[quarter:], far_a2, up)
    from_right_b2 = relay(left_part_b[quarter:], far_b2, down)
    image_grad = finish_images(images_raw, own_sum, images_back)
    text_grad = finish_texts(0, texts_raw, text_own, near, (from_left_a1, from_right_b1))
    text_grad = finish_texts(
        1, texts_raw, text_own, near, (from_left_a2, from_right_b2), text_grad
    )
    return image_grad, text_grad


def solution(mesh):
    spec = P(AXES, None)
    return jax.shard_map(
        body,
        mesh=mesh,
        in_specs=(spec, spec, P(), P()),
        out_specs=(spec, spec),
        check_vma=False,
    )
```

```python
import functools

import jax
import jax.numpy as jnp
from jax import lax
from jax.experimental import pallas as pl
from jax.experimental.pallas import tpu as pltpu
from jax.sharding import PartitionSpec as P

AXES = ("wide", "narrow")
RING = 4
LOG2_E = 1.4426950408889634
MIB = 1024 * 1024
COST = pl.CostEstimate(flops=1000, bytes_accessed=1000, transcendentals=0)
IN_SMEM = pl.BlockSpec(memory_space=pltpu.SMEM)
IN_VMEM = pl.BlockSpec(memory_space=pltpu.VMEM)
IN_HBM = pl.BlockSpec(memory_space=pltpu.HBM)


def ring_route(step, count):
    return [(d, d - d % RING + (d + step) % RING) for d in range(count)]


def line_route(step, count):
    return [(d, (d + step) % count) for d in range(count)]


def send(block, route):
    return lax.ppermute(block, AXES, route)


def after(value, *earlier):
    return lax.optimization_barrier((value, *earlier))[0]


def params(mib):
    return pltpu.CompilerParams(vmem_limit_bytes=mib * MIB)


def like(rows, width, dtype):
    return jax.ShapeDtypeStruct((rows, width), dtype)


def dot(left, right, left_dim, right_dim):
    contract = (((left_dim,), (right_dim,)), ((), ()))
    return lax.dot_general(left, right, contract, preferred_element_type=jnp.float32)


def unit_rows(raw):
    wide = raw.astype(jnp.float32)
    inverse = lax.rsqrt(jnp.sum(wide * wide, axis=-1, keepdims=True) + 1e-06)
    return wide * inverse, inverse


def store_unit_rows(raw_ref, unit_ref, tile):
    for start in range(0, raw_ref.shape[0], tile):
        unit, _ = unit_rows(raw_ref[start : start + tile, :])
        unit_ref[start : start + tile, :] = unit.astype(unit_ref.dtype)


def halves_kernel(texts_ref, first_ref, second_ref, sems):
    half = first_ref.shape[0]
    copies = [
        pltpu.make_async_copy(texts_ref.at[pl.ds(k * half, half)], out, sems.at[k])
        for k, out in enumerate((first_ref, second_ref))
    ]
    for copy in copies:
        copy.start()
    for copy in copies:
        copy.wait()


def halves(texts):
    rows, width = texts.shape
    return pl.pallas_call(
        halves_kernel,
        out_shape=[like(rows // 2, width, texts.dtype)] * 2,
        in_specs=[IN_HBM],
        out_specs=[IN_VMEM] * 2,
        scratch_shapes=[pltpu.SemaphoreType.DMA((2,))],
        compiler_params=params(58),
        cost_estimate=COST,
    )(texts)


def pairs(scalars_ref, texts, images, pieces, weights, low, tile, own=False, arrive=None, leave=None, bases=None):
    scale, bias = scalars_ref[0], scalars_ref[1]
    rate, offset = -LOG2_E * scale, -LOG2_E * bias
    tiles = [(k, start) for k, text in enumerate(texts) for start in range(0, text.shape[0], tile)]
    places = [(piece, start) for piece in pieces for start in range(0, piece.shape[0], tile)]

    def low_rows(i):
        k, start = tiles[i]
        base = i * tile if bases is None else bases[k] + start
        return slice(base, base + tile)

    def exponents(i):
        k, start = tiles[i]
        if start == 0 and arrive is not None:
            arrive(k)
        unit, _ = unit_rows(texts[k][start : start + tile, :])
        unit = unit.astype(jnp.bfloat16)
        low[low_rows(i), :] = unit
        return rate * dot(unit, images(k), 1, 1) + offset

    ahead = exponents(0)
    for i, (k, start) in enumerate(tiles):
        exponent = ahead
        if i + 1 < len(tiles):
            ahead = exponents(i + 1)
        if own:
            row = i * tile + lax.broadcasted_iota(jnp.int32, exponent.shape, 0)
            column = lax.broadcasted_iota(jnp.int32, exponent.shape, 1)
            sign = jnp.where(row == column, -1.0, 1.0)
            weight = (sign / (1.0 + jnp.exp2(sign * exponent))).astype(jnp.bfloat16)
        else:
            weight = (1.0 / (1.0 + jnp.exp2(exponent))).astype(jnp.bfloat16)
        weights[low_rows(i), :] = weight
        product = scale * dot(weight, images(k), 1, 0)
        piece, place = places[i]
        piece[place : place + tile, :] = product.astype(piece.dtype)
        if leave is not None and start + tile == texts[k].shape[0]:
            leave(k)


def own_kernel(tile, scalars_ref, texts_ref, raw_ref, images_ref, partial_ref, sum_ref, *scratch):
    texts, raw, images, low, weights, sems = scratch
    copy = lambda source, target, k: pltpu.make_async_copy(source, target, sems.at[k])
    load_raw, load_texts = copy(raw_ref, raw, 0), copy(texts_ref, texts, 1)
    load_raw.start()
    load_texts.start()
    load_raw.wait()
    store_unit_rows(raw, images, tile)
    store_images = copy(images, images_ref, 0)
    store_images.start()
    load_texts.wait()
    pairs(
        scalars_ref, [texts], lambda k: images[...], [partial_ref], weights, low, tile, own=True
    )

    @pl.loop(0, sum_ref.shape[0] // tile)
    def _(i):
        here = pl.ds(pl.multiple_of(i * tile, tile), tile)
        sum_ref[here, :] = scalars_ref[0] * dot(weights[:, here], low[...], 0, 0)

    store_images.wait()


def own_pair(scalars, texts, raw, tile=256):
    rows, width = raw.shape
    return pl.pallas_call(
        functools.partial(own_kernel, tile),
        out_shape=[
            like(rows, width, jnp.bfloat16),
            like(rows, width, jnp.float32),
            like(rows, width, jnp.float32),
        ],
        in_specs=[IN_SMEM, IN_HBM, IN_HBM],
        out_specs=[IN_HBM, IN_VMEM, IN_VMEM],
        scratch_shapes=[pltpu.VMEM((rows, width), jnp.bfloat16)] * 4
        + [pltpu.VMEM((rows, rows), jnp.bfloat16), pltpu.SemaphoreType.DMA((2,))],
        compiler_params=params(58),
        cost_estimate=COST,
    )(scalars, texts, raw)


def near_kernel(tile, slots_ref, scalars_ref, own_ref, raw_ref, *refs):
    count = (len(refs) - 9) // 2
    sources, pieces = refs[:count], refs[count : 2 * count]
    images_ref, weights_ref, low_ref, images, raw, texts, weights, low, sems = refs[2 * count :]
    half = sources[0].shape[0]
    copy = lambda source, target, k: pltpu.make_async_copy(source, target, sems.at[k])
    load_raw, load_own = copy(raw_ref, raw, 0), copy(own_ref, images.at[0], 1)
    loads = [copy(source, texts.at[k], 2 + k) for k, source in enumerate(sources)]
    for load in (load_raw, load_own, loads[0]):
        load.start()
    load_raw.wait()
    for load in loads[1:]:
        load.start()
    store_unit_rows(raw, images.at[1], tile)
    store_images = copy(images.at[1], images_ref, 0)
    store_images.start()
    load_own.wait()
    stores = []

    def leave(k):
        rows = pl.ds(k * half, half)
        stores.append(copy(weights.at[rows], weights_ref.at[rows], 2 + count + 2 * k))
        stores.append(copy(low.at[rows], low_ref.at[rows], 3 + count + 2 * k))
        for store in stores[-2:]:
            store.start()

    pairs(
        scalars_ref,
        [texts.at[k] for k in range(count)],
        lambda k: images[slots_ref[k]],
        pieces,
        weights,
        low,
        tile,
        arrive=lambda k: loads[k].wait(),
        leave=leave,
    )
    for store in (store_images, *stores):
        store.wait()


def near_pairs(slots, scalars, own_images, raw, texts, tile=256):
    rows, width = raw.shape
    half, count = texts[0].shape[0], len(texts)
    bf16 = jnp.bfloat16
    return pl.pallas_call(
        functools.partial(near_kernel, tile),
        out_shape=[like(half, width, bf16)] * count
        + [like(rows, width, bf16), like(count * half, rows, bf16), like(count * half, width, bf16)],
        in_specs=[IN_SMEM, IN_SMEM] + [IN_HBM] * (2 + count),
        out_specs=[IN_VMEM] * count + [IN_HBM] * 3,
        scratch_shapes=[
            pltpu.VMEM((2, rows, width), bf16),
            pltpu.VMEM((rows, width), bf16),
            pltpu.VMEM((count, half, width), bf16),
            pltpu.VMEM((count * half, rows), bf16),
            pltpu.VMEM((count * half, width), bf16),
            pltpu.SemaphoreType.DMA((2 + 3 * count,)),
        ],
        compiler_params=params(58),
        cost_estimate=COST,
    )(slots, scalars, own_images, raw, *texts)


def pair_sums_kernel(tile, slots_ref, scalars_ref, own_ref, next_ref, sum_ref, *refs):
    weights_ref, low_ref = refs[:2]
    sources, pieces = refs[2:4], refs[4:8]
    sums_ref, images, texts, weights, low, sums, sems = refs[8:]
    half = sources[0].shape[0]
    scale = scalars_ref[0]
    copy = lambda source, target, k: pltpu.make_async_copy(source, target, sems.at[k])
    load_images = [copy(own_ref, images.at[k], k) for k in range(2)]
    load_next = [copy(next_ref, images.at[k], k) for k in range(2)]
    load_texts = [copy(ref, texts.at[k], 2 + k) for k, ref in enumerate(sources)]

    def start_images(k):
        pl.when(slots_ref[k] == 0)(load_images[k].start)
        pl.when(slots_ref[k] != 0)(load_next[k].start)

    spans = [pl.ds(k * half, half) for k in range(4)]
    load_rest = [copy(sum_ref, sums.at[0], 4)]
    for k, (source, target) in enumerate(((0, 3), (1, 1))):
        load_rest.append(copy(weights_ref.at[spans[source]], weights.at[spans[target]], 5 + 2 * k))
        load_rest.append(copy(low_ref.at[spans[source]], low.at[spans[target]], 6 + 2 * k))
    start_images(0)
    load_texts[0].start()
    load_images[0].wait()
    start_images(1)
    for load in (load_texts[1], *load_rest):
        load.start()

    def arrive(k):
        load_texts[k].wait()
        if k == 1:
            load_images[1].wait()

    pairs(
        scalars_ref,
        [texts.at[k] for k in range(2)],
        lambda k: images[k],
        pieces,
        weights,
        low,
        tile,
        arrive=arrive,
        bases=(0, 2 * half),
    )
    sums[1] = jnp.zeros(sums.shape[1:], jnp.float32)
    for load in load_rest:
        load.wait()
    count = sums.shape[1] // tile

    def store(i):
        part = pl.ds(pl.multiple_of(i * tile, tile), tile)
        return copy(sums.at[:, part], sums_ref.at[:, part], i)

    @pl.loop(0, count)
    def _(i):
        part = pl.ds(pl.multiple_of(i * tile, tile), tile)
        for k in range(2):
            rows = slice(2 * k * half, 2 * (k + 1) * half)
            sums[slots_ref[k], part, :] += scale * dot(weights[rows, part], low[rows, :], 0, 0)
        store(i).start()

    for i in range(count):
        store(i).wait()


def pair_sums(slots, scalars, own_images, next_images, own, weights, low, texts, tile=256):
    rows, width = own.shape
    half = texts[0].shape[0]
    bf16 = jnp.bfloat16
    return pl.pallas_call(
        functools.partial(pair_sums_kernel, tile),
        out_shape=[like(half // 2, width, bf16)] * 4
        + [jax.ShapeDtypeStruct((2, rows, width), jnp.float32)],
        in_specs=[IN_SMEM, IN_SMEM] + [IN_HBM] * 7,
        out_specs=[IN_VMEM] * 4 + [IN_HBM],
        scratch_shapes=[
            pltpu.VMEM((2, rows, width), bf16),
            pltpu.VMEM((2, half, width), bf16),
            pltpu.VMEM((4 * half, rows), bf16),
            pltpu.VMEM((4 * half, width), bf16),
            pltpu.VMEM((2, rows, width), jnp.float32),
            pltpu.SemaphoreType.DMA((9,)),
        ],
        compiler_params=params(58),
        cost_estimate=COST,
    )(slots, scalars, own_images, next_images, own, weights, low, *texts)


def far_kernel(tile, slot_ref, scalars_ref, own_ref, next_ref, sums_ref, *refs):
    sources, pieces = refs[:2], refs[2:6]
    total_ref, ready_ref, images, texts, weights, low, sums, sems = refs[6:]
    copy = lambda source, target, k: pltpu.make_async_copy(source, target, sems.at[k])
    load_own, load_next = copy(own_ref, images, 0), copy(next_ref, images, 0)
    loads = [copy(source, texts.at[k], 1 + k) for k, source in enumerate(sources)]
    load_sums = copy(sums_ref, sums, 3)
    pl.when(slot_ref[0] == 0)(load_own.start)
    pl.when(slot_ref[0] != 0)(load_next.start)
    loads[0].start()
    load_own.wait()
    loads[1].start()
    load_sums.start()
    pairs(
        scalars_ref,
        [texts.at[k] for k in range(2)],
        lambda k: images[...],
        pieces,
        weights,
        low,
        tile,
        arrive=lambda k: loads[k].wait(),
    )
    load_sums.wait()
    next_share = scalars_ref[0] * slot_ref[0].astype(jnp.float32)
    own_share = scalars_ref[0] - next_share
    count = sums.shape[1] // tile

    def store(i):
        part = pl.ds(pl.multiple_of(i * tile, tile), tile)
        return copy(sums.at[0, part], total_ref.at[part], i)

    @pl.loop(0, count)
    def _(i):
        part = pl.ds(pl.multiple_of(i * tile, tile), tile)
        product = dot(weights[:, part], low[...], 0, 0)
        ready_ref[part, :] = (sums[1, part, :] + next_share * product).astype(ready_ref.dtype)
        sums[0, part, :] += own_share * product
        store(i).start()

    for i in range(count):
        store(i).wait()


def far_pair(slot, scalars, own_images, next_images, sums, texts, tile=256):
    rows, width = own_images.shape
    half = texts[0].shape[0]
    bf16 = jnp.bfloat16
    return pl.pallas_call(
        functools.partial(far_kernel, tile),
        out_shape=[like(half // 2, width, bf16)] * 4
        + [like(rows, width, jnp.float32), like(rows, width, bf16)],
        in_specs=[IN_SMEM, IN_SMEM] + [IN_HBM] * 5,
        out_specs=[IN_VMEM] * 4 + [IN_HBM, IN_VMEM],
        scratch_shapes=[
            pltpu.VMEM((rows, width), bf16),
            pltpu.VMEM((2, half, width), bf16),
            pltpu.VMEM((2 * half, rows), bf16),
            pltpu.VMEM((2 * half, width), bf16),
            pltpu.VMEM((2, rows, width), jnp.float32),
            pltpu.SemaphoreType.DMA((4,)),
        ],
        compiler_params=params(58),
        cost_estimate=COST,
    )(slot, scalars, own_images, next_images, sums, *texts)


def finish_rows(raw, direction):
    unit, inverse = unit_rows(raw)
    inner = jnp.sum(unit * direction, axis=-1, keepdims=True)
    return inverse * (direction - unit * inner)


def finish_images_kernel(raw_ref, own_ref, back_ref, grad_ref):
    direction = own_ref[...] + back_ref[...].astype(jnp.float32)
    grad_ref[...] = finish_rows(raw_ref[...], direction)


def finish_images(raw, own, back):
    rows, width = raw.shape
    tile = rows // 2
    flat = pl.BlockSpec((tile, width), lambda i: (i, 0))
    return pl.pallas_call(
        finish_images_kernel,
        grid=(rows // tile,),
        out_shape=jax.ShapeDtypeStruct((rows, width), jnp.float32),
        in_specs=[flat] * 3,
        out_specs=flat,
        compiler_params=params(14),
        cost_estimate=COST,
    )(raw, own, back)


def finish_texts_kernel(phase, raw_ref, own_ref, *refs):
    halves_refs, quarter_refs, grad_ref = refs[:2], refs[2:4], refs[-1]
    rows = raw_ref.shape[0]
    for step in range(2):

        @pl.when(pl.program_id(0) == step)
        def _():
            near = halves_refs[step][phase * rows : (phase + 1) * rows, :]
            direction = own_ref[...] + near.astype(jnp.float32)
            direction = direction + quarter_refs[step][...].astype(jnp.float32)
            grad_ref[...] = finish_rows(raw_ref[...], direction)


def finish_texts(phase, raw, own, halves_in, quarters_in, held=None):
    rows, width = raw.shape
    flat = pl.BlockSpec((rows // 4, width), lambda i: (2 * i + phase, 0))
    aliased = [] if held is None else [held]
    return pl.pallas_call(
        functools.partial(finish_texts_kernel, phase),
        grid=(2,),
        out_shape=jax.ShapeDtypeStruct((rows, width), jnp.float32),
        in_specs=[flat] * 2
        + [IN_VMEM] * 4
        + [pl.BlockSpec(memory_space=pl.ANY)] * len(aliased),
        out_specs=flat,
        input_output_aliases={} if held is None else {6: 0},
        compiler_params=params(14),
        cost_estimate=COST,
    )(raw, own, *halves_in, *quarters_in, *aliased)


def body(images_raw, texts_raw, inverse_softness, additive_shift_term):
    count = lax.axis_size("wide") * lax.axis_size("narrow")
    z = lax.axis_index("narrow") % RING
    scalars = jnp.concatenate([inverse_softness, additive_shift_term])
    slot = [jnp.where(z < RING - t, 1, 0).astype(jnp.int32).reshape(1) for t in range(RING)]
    slots = lambda *places: jnp.concatenate([slot[t] for t in places])
    up, down = ring_route(1, count), ring_route(-1, count)

    images_next_raw = send(images_raw, line_route(-RING, count))
    own_a, own_b = halves(texts_raw)
    left_a = send(own_a, up)
    right_b = send(own_b, down)
    images, text_own, own_sum = own_pair(scalars, texts_raw, images_raw)
    left_b = send(after(own_b, own_sum), up)
    right_a = send(after(own_a, own_sum), down)
    far_a = send(left_a, up)
    far_b = send(right_b, down)

    left_part_a, right_part_b, images_next, weights, low = near_pairs(
        slots(3, 1), scalars, images, images_next_raw, [left_a, right_b]
    )
    from_right_a = send(left_part_a, down)
    from_left_b = send(right_part_b, up)
    right_a1, right_a2, left_b1, left_b2, sums = pair_sums(
        slots(1, 3), scalars, images, images_next, own_sum, weights, low, [right_a, left_b]
    )
    *far_parts, own_sum, next_sum = far_pair(
        slots(2), scalars, images, images_next, sums, [far_a, far_b]
    )
    far_a1, far_b1 = send(far_parts[0], up), send(far_parts[2], down)
    images_back = send(next_sum, line_route(RING, count))
    near = (from_right_a, from_left_b)
    far_a2 = send(after(far_parts[1], next_sum, *near), up)
    far_b2 = send(after(far_parts[3], next_sum, *near), down)

    def relay(part, far, route):
        total = after(part, own_sum).astype(jnp.float32) + far.astype(jnp.float32)
        return send(total.astype(jnp.bfloat16), route)

    from_left_a1 = relay(right_a1, far_a1, up)
    from_right_b1 = relay(left_b1, far_b1, down)
    from_left_a2 = relay(right_a2, far_a2, up)
    from_right_b2 = relay(left_b2, far_b2, down)
    image_grad = finish_images(images_raw, own_sum, images_back)
    text_grad = finish_texts(0, texts_raw, text_own, near, (from_left_a1, from_right_b1))
    text_grad = finish_texts(
        1, after(texts_raw, image_grad), text_own, near, (from_left_a2, from_right_b2), text_grad
    )
    return image_grad, text_grad


def solution(mesh):
    spec = P(AXES, None)
    return jax.shard_map(
        body,
        mesh=mesh,
        in_specs=(spec, spec, P(), P()),
        out_specs=(spec, spec),
        check_vma=False,
    )
```

```python
import functools

import jax
import jax.numpy as jnp
from jax import lax
from jax.experimental import pallas as pl
from jax.experimental.pallas import tpu as pltpu
from jax.sharding import PartitionSpec as P

AXES = ("wide", "narrow")
RING = 4
LOG2_E = 1.4426950408889634
MIB = 1024 * 1024
COST = pl.CostEstimate(flops=1000, bytes_accessed=1000, transcendentals=0)
IN_SMEM = pl.BlockSpec(memory_space=pltpu.SMEM)
IN_VMEM = pl.BlockSpec(memory_space=pltpu.VMEM)
IN_HBM = pl.BlockSpec(memory_space=pltpu.HBM)


def ring_route(step, count):
    return [(d, d - d % RING + (d + step) % RING) for d in range(count)]


def line_route(step, count):
    return [(d, (d + step) % count) for d in range(count)]


def send(block, route):
    return lax.ppermute(block, AXES, route)


def after(value, *earlier):
    return lax.optimization_barrier((value, *earlier))[0]


def params(mib):
    return pltpu.CompilerParams(vmem_limit_bytes=mib * MIB)


def like(rows, width, dtype):
    return jax.ShapeDtypeStruct((rows, width), dtype)


def dot(left, right, left_dim, right_dim):
    contract = (((left_dim,), (right_dim,)), ((), ()))
    return lax.dot_general(left, right, contract, preferred_element_type=jnp.float32)


def unit_rows(raw):
    wide = raw.astype(jnp.float32)
    inverse = lax.rsqrt(jnp.sum(wide * wide, axis=-1, keepdims=True) + 1e-06)
    return wide * inverse, inverse


def store_unit_rows(raw_ref, unit_ref, tile):
    for start in range(0, raw_ref.shape[0], tile):
        unit, _ = unit_rows(raw_ref[start : start + tile, :])
        unit_ref[start : start + tile, :] = unit.astype(unit_ref.dtype)


def halves_kernel(texts_ref, first_ref, second_ref, chunks, sems):
    count, rows = chunks.shape[:2]
    loads = [
        pltpu.make_async_copy(texts_ref.at[pl.ds(k * rows, rows)], chunks.at[k], sems.at[k])
        for k in range(count)
    ]
    stores = []
    for k in range(count):
        out = first_ref if 2 * k < count else second_ref
        place = out.at[pl.ds(k % (count // 2) * rows, rows)]
        stores.append(pltpu.make_async_copy(chunks.at[k], place, sems.at[count + k]))
    for load in loads:
        load.start()
    for load, store in zip(loads, stores):
        load.wait()
        store.start()
    for store in stores:
        store.wait()


def halves(texts):
    rows, width = texts.shape
    return pl.pallas_call(
        halves_kernel,
        out_shape=[like(rows // 2, width, texts.dtype)] * 2,
        in_specs=[IN_HBM],
        out_specs=[IN_HBM] * 2,
        scratch_shapes=[
            pltpu.VMEM((4, rows // 4, width), texts.dtype),
            pltpu.SemaphoreType.DMA((8,)),
        ],
        compiler_params=params(58),
        cost_estimate=COST,
    )(texts)


def cut_rows(half):
    return [half // 2, half // 2]


def pairs(scalars_ref, texts, images, pieces, weights, low, tile, own=False, arrive=None, leave=None, bases=None):
    scale, bias = scalars_ref[0], scalars_ref[1]
    rate, offset = -LOG2_E * scale, -LOG2_E * bias
    tiles = [(k, start) for k, text in enumerate(texts) for start in range(0, text.shape[0], tile)]
    places = [(piece, start) for piece in pieces for start in range(0, piece.shape[0], tile)]

    def low_rows(i):
        k, start = tiles[i]
        base = i * tile if bases is None else bases[k] + start
        return slice(base, base + tile)

    def exponents(i):
        k, start = tiles[i]
        if start == 0 and arrive is not None:
            arrive(k)
        unit, _ = unit_rows(texts[k][start : start + tile, :])
        unit = unit.astype(jnp.bfloat16)
        low[low_rows(i), :] = unit
        return rate * dot(unit, images(k), 1, 1) + offset

    ahead = exponents(0)
    for i, (k, start) in enumerate(tiles):
        exponent = ahead
        if i + 1 < len(tiles):
            ahead = exponents(i + 1)
        if own:
            row = i * tile + lax.broadcasted_iota(jnp.int32, exponent.shape, 0)
            column = lax.broadcasted_iota(jnp.int32, exponent.shape, 1)
            sign = jnp.where(row == column, -1.0, 1.0)
            weight = (sign / (1.0 + jnp.exp2(sign * exponent))).astype(jnp.bfloat16)
        else:
            weight = (1.0 / (1.0 + jnp.exp2(exponent))).astype(jnp.bfloat16)
        weights[low_rows(i), :] = weight
        product = scale * dot(weight, images(k), 1, 0)
        piece, place = places[i]
        piece[place : place + tile, :] = product.astype(piece.dtype)
        if leave is not None and start + tile == texts[k].shape[0]:
            leave(k)


def own_kernel(tile, scalars_ref, texts_ref, raw_ref, images_ref, partial_ref, sum_ref, *scratch):
    texts, raw, images, low, weights, sems = scratch
    copy = lambda source, target, k: pltpu.make_async_copy(source, target, sems.at[k])
    load_raw, load_texts = copy(raw_ref, raw, 0), copy(texts_ref, texts, 1)
    load_raw.start()
    load_texts.start()
    load_raw.wait()
    store_unit_rows(raw, images, tile)
    store_images = copy(images, images_ref, 0)
    store_images.start()
    load_texts.wait()
    pairs(
        scalars_ref, [texts], lambda k: images[...], [partial_ref], weights, low, tile, own=True
    )

    @pl.loop(0, sum_ref.shape[0] // tile)
    def _(i):
        here = pl.ds(pl.multiple_of(i * tile, tile), tile)
        sum_ref[here, :] = scalars_ref[0] * dot(weights[:, here], low[...], 0, 0)

    store_images.wait()


def own_pair(scalars, texts, raw, tile=256):
    rows, width = raw.shape
    return pl.pallas_call(
        functools.partial(own_kernel, tile),
        out_shape=[
            like(rows, width, jnp.bfloat16),
            like(rows, width, jnp.float32),
            like(rows, width, jnp.float32),
        ],
        in_specs=[IN_SMEM, IN_HBM, IN_HBM],
        out_specs=[IN_HBM, IN_VMEM, IN_VMEM],
        scratch_shapes=[pltpu.VMEM((rows, width), jnp.bfloat16)] * 4
        + [pltpu.VMEM((rows, rows), jnp.bfloat16), pltpu.SemaphoreType.DMA((2,))],
        compiler_params=params(58),
        cost_estimate=COST,
    )(scalars, texts, raw)


def near_kernel(tile, slots_ref, scalars_ref, own_ref, raw_ref, *refs):
    count = (len(refs) - 10) // 2
    sources, outs = refs[:count], refs[count : 2 * count]
    images_ref, weights_ref, low_ref, images, raw, texts, pieces, weights, low, sems = refs[
        2 * count :
    ]
    half = sources[0].shape[0]
    copy = lambda source, target, k: pltpu.make_async_copy(source, target, sems.at[k])
    load_own = copy(own_ref, images.at[0], 1)
    loads = [copy(source, texts.at[k], 2 + k) for k, source in enumerate(sources)]
    load_raw = copy(raw_ref, raw, 0)
    for load in (load_raw, load_own, loads[0]):
        load.start()
    load_raw.wait()
    for load in loads[1:]:
        load.start()
    store_unit_rows(raw, images.at[1], tile)
    store_images = copy(images.at[1], images_ref, 0)
    store_images.start()
    load_own.wait()
    stores = []

    def leave(k):
        rows = pl.ds(k * half, half)
        first = 2 + count + 3 * k
        stores.append(copy(pieces.at[k], outs[k], first))
        stores.append(copy(weights.at[rows], weights_ref.at[rows], first + 1))
        stores.append(copy(low.at[rows], low_ref.at[rows], first + 2))
        for store in stores[-3:]:
            store.start()

    pairs(
        scalars_ref,
        [texts.at[k] for k in range(count)],
        lambda k: images[slots_ref[k]],
        [pieces.at[k] for k in range(count)],
        weights,
        low,
        tile,
        arrive=lambda k: loads[k].wait(),
        leave=leave,
    )
    for store in (store_images, *stores):
        store.wait()


def near_pairs(slots, scalars, own_images, raw, texts, tile=256):
    rows, width = raw.shape
    half, count = texts[0].shape[0], len(texts)
    bf16 = jnp.bfloat16
    return pl.pallas_call(
        functools.partial(near_kernel, tile),
        out_shape=[like(half, width, bf16)] * count
        + [like(rows, width, bf16), like(count * half, rows, bf16), like(count * half, width, bf16)],
        in_specs=[IN_SMEM, IN_SMEM] + [IN_HBM] * (2 + count),
        out_specs=[IN_HBM] * (count + 3),
        scratch_shapes=[
            pltpu.VMEM((2, rows, width), bf16),
            pltpu.VMEM((rows, width), bf16),
            pltpu.VMEM((count, half, width), bf16),
            pltpu.VMEM((count, half, width), bf16),
            pltpu.VMEM((count * half, rows), bf16),
            pltpu.VMEM((count * half, width), bf16),
            pltpu.SemaphoreType.DMA((2 + 4 * count,)),
        ],
        compiler_params=params(58),
        cost_estimate=COST,
    )(slots, scalars, own_images, raw, *texts)


def pair_sums_kernel(tile, slots_ref, scalars_ref, own_ref, next_ref, sum_ref, *refs):
    weights_ref, low_ref = refs[:2]
    sources, outs = refs[2:4], refs[4:8]
    sums_ref, images, texts, pieces, weights, low, sums, sems = refs[8:]
    half = sources[0].shape[0]
    scale = scalars_ref[0]
    copy = lambda source, target, k: pltpu.make_async_copy(source, target, sems.at[k])
    load_images = [copy(own_ref, images.at[k], k) for k in range(2)]
    load_next = [copy(next_ref, images.at[k], k) for k in range(2)]
    load_texts = [copy(ref, texts.at[k], 2 + k) for k, ref in enumerate(sources)]

    def start_images(k):
        pl.when(slots_ref[k] == 0)(load_images[k].start)
        pl.when(slots_ref[k] != 0)(load_next[k].start)

    spans = [pl.ds(k * half, half) for k in range(4)]
    load_rest = [copy(sum_ref, sums.at[0], 4)]
    for k, (source, target) in enumerate(((0, 3), (1, 1))):
        load_rest.append(copy(weights_ref.at[spans[source]], weights.at[spans[target]], 5 + 2 * k))
        load_rest.append(copy(low_ref.at[spans[source]], low.at[spans[target]], 6 + 2 * k))
    start_images(0)
    load_texts[0].start()
    load_images[0].wait()
    start_images(1)
    for load in (load_texts[1], *load_rest):
        load.start()

    def arrive(k):
        load_texts[k].wait()
        if k == 1:
            load_images[1].wait()

    cuts = [
        copy(pieces.at[i // 2, pl.ds(i % 2 * outs[0].shape[0], out.shape[0])], out, 9 + i)
        for i, out in enumerate(outs)
    ]

    def leave(k):
        for cut in cuts[2 * k : 2 * k + 2]:
            cut.start()

    pairs(
        scalars_ref,
        [texts.at[k] for k in range(2)],
        lambda k: images[k],
        [pieces.at[k] for k in range(2)],
        weights,
        low,
        tile,
        arrive=arrive,
        leave=leave,
        bases=(0, 2 * half),
    )
    sums[1] = jnp.zeros(sums.shape[1:], jnp.float32)
    for load in load_rest:
        load.wait()
    count = sums.shape[1] // tile

    def store(i):
        part = pl.ds(pl.multiple_of(i * tile, tile), tile)
        return copy(sums.at[:, part], sums_ref.at[:, part], i)

    @pl.loop(0, count)
    def _(i):
        part = pl.ds(pl.multiple_of(i * tile, tile), tile)
        for k in range(2):
            rows = slice(2 * k * half, 2 * (k + 1) * half)
            sums[slots_ref[k], part, :] += scale * dot(weights[rows, part], low[rows, :], 0, 0)
        store(i).start()

    for i in range(count):
        store(i).wait()
    for cut in cuts:
        cut.wait()


def pair_sums(slots, scalars, own_images, next_images, own, weights, low, texts, tile=256):
    rows, width = own.shape
    half = texts[0].shape[0]
    bf16 = jnp.bfloat16
    return pl.pallas_call(
        functools.partial(pair_sums_kernel, tile),
        out_shape=[like(size, width, bf16) for size in cut_rows(half) * 2]
        + [jax.ShapeDtypeStruct((2, rows, width), jnp.float32)],
        in_specs=[IN_SMEM, IN_SMEM] + [IN_HBM] * 7,
        out_specs=[IN_HBM] * 5,
        scratch_shapes=[
            pltpu.VMEM((2, rows, width), bf16),
            pltpu.VMEM((2, half, width), bf16),
            pltpu.VMEM((2, half, width), bf16),
            pltpu.VMEM((4 * half, rows), bf16),
            pltpu.VMEM((4 * half, width), bf16),
            pltpu.VMEM((2, rows, width), jnp.float32),
            pltpu.SemaphoreType.DMA((13,)),
        ],
        compiler_params=params(58),
        cost_estimate=COST,
    )(slots, scalars, own_images, next_images, own, weights, low, *texts)


def far_kernel(tile, slot_ref, scalars_ref, own_ref, next_ref, sums_ref, *refs):
    sources, outs = refs[:2], refs[2:6]
    total_ref, ready_ref, images, texts, pieces, weights, low, sums, ready, sems = refs[6:]
    half = sources[0].shape[0]
    copy = lambda source, target, k: pltpu.make_async_copy(source, target, sems.at[k])
    load_own, load_next = copy(own_ref, images, 0), copy(next_ref, images, 0)
    loads = [copy(source, texts.at[k], 1 + k) for k, source in enumerate(sources)]
    load_sums = copy(sums_ref, sums, 3)
    pl.when(slot_ref[0] == 0)(load_own.start)
    pl.when(slot_ref[0] != 0)(load_next.start)
    loads[0].start()
    load_own.wait()
    loads[1].start()
    load_sums.start()
    cuts = [
        copy(pieces.at[i // 2, pl.ds(i % 2 * outs[0].shape[0], out.shape[0])], out, 8 + i)
        for i, out in enumerate(outs)
    ]

    def leave(k):
        for cut in cuts[2 * k : 2 * k + 2]:
            cut.start()

    pairs(
        scalars_ref,
        [texts.at[k] for k in range(2)],
        lambda k: images[...],
        [pieces.at[k] for k in range(2)],
        weights,
        low,
        tile,
        arrive=lambda k: loads[k].wait(),
        leave=leave,
    )
    load_sums.wait()
    next_share = scalars_ref[0] * slot_ref[0].astype(jnp.float32)
    own_share = scalars_ref[0] - next_share
    count = sums.shape[1] // tile

    def stores(i):
        part = pl.ds(pl.multiple_of(i * tile, tile), tile)
        return (
            copy(ready.at[part], ready_ref.at[part], 4 + i),
            copy(sums.at[0, part], total_ref.at[part], i),
        )

    @pl.loop(0, count)
    def _(i):
        part = pl.ds(pl.multiple_of(i * tile, tile), tile)
        product = dot(weights[:, part], low[...], 0, 0)
        ready[part, :] = (sums[1, part, :] + next_share * product).astype(ready.dtype)
        sums[0, part, :] += own_share * product
        for store in stores(i):
            store.start()

    for i in range(count):
        for store in stores(i):
            store.wait()
    for cut in cuts:
        cut.wait()


def far_pair(slot, scalars, own_images, next_images, sums, texts, tile=256):
    rows, width = own_images.shape
    half = texts[0].shape[0]
    bf16 = jnp.bfloat16
    return pl.pallas_call(
        functools.partial(far_kernel, tile),
        out_shape=[like(size, width, bf16) for size in cut_rows(half) * 2]
        + [like(rows, width, jnp.float32), like(rows, width, bf16)],
        in_specs=[IN_SMEM, IN_SMEM] + [IN_HBM] * 5,
        out_specs=[IN_HBM] * 6,
        scratch_shapes=[
            pltpu.VMEM((rows, width), bf16),
            pltpu.VMEM((2, half, width), bf16),
            pltpu.VMEM((2, half, width), bf16),
            pltpu.VMEM((2 * half, rows), bf16),
            pltpu.VMEM((2 * half, width), bf16),
            pltpu.VMEM((2, rows, width), jnp.float32),
            pltpu.VMEM((rows, width), bf16),
            pltpu.SemaphoreType.DMA((12,)),
        ],
        compiler_params=params(58),
        cost_estimate=COST,
    )(slot, scalars, own_images, next_images, sums, *texts)


def finish_rows(raw, direction):
    unit, inverse = unit_rows(raw)
    inner = jnp.sum(unit * direction, axis=-1, keepdims=True)
    return inverse * (direction - unit * inner)


def finish_images_kernel(raw_ref, own_ref, back_ref, grad_ref):
    direction = own_ref[...] + back_ref[...].astype(jnp.float32)
    grad_ref[...] = finish_rows(raw_ref[...], direction)


def finish_images(raw, own, back):
    rows, width = raw.shape
    tile = rows // 2
    flat = pl.BlockSpec((tile, width), lambda i: (i, 0))
    return pl.pallas_call(
        finish_images_kernel,
        grid=(rows // tile,),
        out_shape=jax.ShapeDtypeStruct((rows, width), jnp.float32),
        in_specs=[flat] * 3,
        out_specs=flat,
        compiler_params=params(14),
        cost_estimate=COST,
    )(raw, own, back)


def first_texts_kernel(raw_ref, own_ref, *refs):
    near_refs, last_refs, grad_ref = refs[:2], refs[2:4], refs[4]
    rows = raw_ref.shape[0]
    for half in range(2):

        @pl.when(pl.program_id(0) == half)
        def _():
            direction = own_ref[...] + near_refs[half][:rows, :].astype(jnp.float32)
            direction = direction + last_refs[half][...].astype(jnp.float32)
            grad_ref[...] = finish_rows(raw_ref[...], direction)


def finish_first_texts(raw, own, near, last):
    rows, width = raw.shape
    flat = pl.BlockSpec((rows // 4, width), lambda i: (2 * i, 0))
    return pl.pallas_call(
        first_texts_kernel,
        grid=(2,),
        out_shape=like(rows, width, jnp.float32),
        in_specs=[flat] * 2 + [IN_VMEM] * 4,
        out_specs=flat,
        compiler_params=params(14),
        cost_estimate=COST,
    )(raw, own, *near, *last)


def gather_kernel(raw_ref, own_ref, *refs):
    near_refs, (rows_ref, base_ref) = refs[:2], refs[2:]
    rows = raw_ref.shape[0]
    rows_ref[...] = raw_ref[...]
    for half in range(2):

        @pl.when(pl.program_id(0) == half)
        def _():
            base_ref[...] = own_ref[...] + near_refs[half][rows:, :].astype(jnp.float32)


def gather_last_texts(raw, own, near):
    rows, width = raw.shape
    flat = pl.BlockSpec((rows // 4, width), lambda i: (2 * i + 1, 0))
    out = pl.BlockSpec((rows // 4, width), lambda i: (i, 0))
    return pl.pallas_call(
        gather_kernel,
        grid=(2,),
        out_shape=[like(rows // 2, width, raw.dtype), like(rows // 2, width, jnp.float32)],
        in_specs=[flat] * 2 + [IN_VMEM] * 2,
        out_specs=[out] * 2,
        compiler_params=params(14),
        cost_estimate=COST,
    )(raw, own, *near)


def last_texts_kernel(raw_ref, base_ref, *refs):
    last_refs, grad_ref = refs[:2], refs[-1]
    rows = grad_ref.shape[0]
    for half in range(2):

        @pl.when(pl.program_id(0) == half)
        def _():
            here = slice(half * rows, (half + 1) * rows)
            direction = base_ref[here, :] + last_refs[half][...].astype(jnp.float32)
            grad_ref[...] = finish_rows(raw_ref[here, :], direction)


def finish_last_texts(raw, base, last, held):
    rows, width = held.shape
    return pl.pallas_call(
        last_texts_kernel,
        grid=(2,),
        out_shape=like(rows, width, jnp.float32),
        in_specs=[IN_VMEM] * 4 + [pl.BlockSpec(memory_space=pl.ANY)],
        out_specs=pl.BlockSpec((rows // 4, width), lambda i: (2 * i + 1, 0)),
        input_output_aliases={4: 0},
        compiler_params=params(14),
        cost_estimate=COST,
    )(raw, base, *last, held)


def body(images_raw, texts_raw, inverse_softness, additive_shift_term):
    count = lax.axis_size("wide") * lax.axis_size("narrow")
    z = lax.axis_index("narrow") % RING
    scalars = jnp.concatenate([inverse_softness, additive_shift_term])
    slot = [jnp.where(z < RING - t, 1, 0).astype(jnp.int32).reshape(1) for t in range(RING)]
    slots = lambda *places: jnp.concatenate([slot[t] for t in places])
    up, down = ring_route(1, count), ring_route(-1, count)

    images_next_raw = send(images_raw, line_route(-RING, count))
    own_a, own_b = halves(texts_raw)
    left_a = send(own_a, up)
    right_b = send(own_b, down)
    images, text_own, own_sum = own_pair(scalars, texts_raw, images_raw)
    left_b = send(after(own_b, own_sum), up)
    right_a = send(after(own_a, own_sum), down)
    far_a = send(left_a, up)
    far_b = send(right_b, down)

    left_part_a, right_part_b, images_next, weights, low = near_pairs(
        slots(3, 1), scalars, images, images_next_raw, [left_a, right_b]
    )
    from_right_a = send(left_part_a, down)
    from_left_b = send(right_part_b, up)
    right_a1, right_a2, left_b1, left_b2, sums = pair_sums(
        slots(1, 3), scalars, images, images_next, own_sum, weights, low, [right_a, left_b]
    )
    *far_parts, own_sum, next_sum = far_pair(
        slots(2), scalars, images, images_next, sums, [far_a, far_b]
    )
    far_a1, far_b1 = send(far_parts[0], up), send(far_parts[2], down)
    images_back = send(next_sum, line_route(RING, count))
    near = (from_right_a, from_left_b)
    far_a2 = send(after(far_parts[1], next_sum, *near), up)
    far_b2 = send(after(far_parts[3], next_sum, *near), down)

    rows_last, base_last = gather_last_texts(texts_raw, text_own, near)

    def relay(part, far, route):
        total = after(part, own_sum, base_last).astype(jnp.float32) + far.astype(jnp.float32)
        return send(total.astype(jnp.bfloat16), route)

    from_left_a1 = relay(right_a1, far_a1, up)
    from_right_b1 = relay(left_b1, far_b1, down)
    from_left_a2 = relay(right_a2, far_a2, up)
    from_right_b2 = relay(left_b2, far_b2, down)
    image_grad = finish_images(images_raw, own_sum, images_back)
    text_grad = finish_first_texts(texts_raw, text_own, near, (from_left_a1, from_right_b1))
    text_grad = finish_last_texts(
        rows_last, after(base_last, image_grad), (from_left_a2, from_right_b2), text_grad
    )
    return image_grad, text_grad


def solution(mesh):
    spec = P(AXES, None)
    return jax.shard_map(
        body,
        mesh=mesh,
        in_specs=(spec, spec, P(), P()),
        out_specs=(spec, spec),
        check_vma=False,
    )
```

```python
import functools

import jax
import jax.numpy as jnp
from jax import lax
from jax.experimental import pallas as pl
from jax.experimental.pallas import tpu as pltpu
from jax.sharding import PartitionSpec as P

AXES = ("wide", "narrow")
RING = 4
LOG2_E = 1.4426950408889634
MIB = 1024 * 1024
COST = pl.CostEstimate(flops=1000, bytes_accessed=1000, transcendentals=0)
IN_SMEM = pl.BlockSpec(memory_space=pltpu.SMEM)
IN_VMEM = pl.BlockSpec(memory_space=pltpu.VMEM)
IN_HBM = pl.BlockSpec(memory_space=pltpu.HBM)


def ring_route(step, count):
    return [(d, d - d % RING + (d + step) % RING) for d in range(count)]


def line_route(step, count):
    return [(d, (d + step) % count) for d in range(count)]


def send(block, route):
    return lax.ppermute(block, AXES, route)


def after(value, *earlier):
    return lax.optimization_barrier((value, *earlier))[0]


def params(mib):
    return pltpu.CompilerParams(vmem_limit_bytes=mib * MIB)


def like(rows, width, dtype):
    return jax.ShapeDtypeStruct((rows, width), dtype)


def dot(left, right, left_dim, right_dim):
    contract = (((left_dim,), (right_dim,)), ((), ()))
    return lax.dot_general(left, right, contract, preferred_element_type=jnp.float32)


def unit_rows(raw):
    wide = raw.astype(jnp.float32)
    inverse = lax.rsqrt(jnp.sum(wide * wide, axis=-1, keepdims=True) + 1e-06)
    return wide * inverse, inverse


def store_unit_rows(raw_ref, unit_ref, tile):
    for start in range(0, raw_ref.shape[0], tile):
        unit, _ = unit_rows(raw_ref[start : start + tile, :])
        unit_ref[start : start + tile, :] = unit.astype(unit_ref.dtype)


def halves_kernel(texts_ref, first_ref, second_ref, chunks, sems):
    count, rows = chunks.shape[:2]
    loads = [
        pltpu.make_async_copy(texts_ref.at[pl.ds(k * rows, rows)], chunks.at[k], sems.at[k])
        for k in range(count)
    ]
    stores = []
    for k in range(count):
        out = first_ref if 2 * k < count else second_ref
        place = out.at[pl.ds(k % (count // 2) * rows, rows)]
        stores.append(pltpu.make_async_copy(chunks.at[k], place, sems.at[count + k]))
    for load in loads:
        load.start()
    for load, store in zip(loads, stores):
        load.wait()
        store.start()
    for store in stores:
        store.wait()


def halves(texts):
    rows, width = texts.shape
    return pl.pallas_call(
        halves_kernel,
        out_shape=[like(rows // 2, width, texts.dtype)] * 2,
        in_specs=[IN_HBM],
        out_specs=[IN_HBM] * 2,
        scratch_shapes=[
            pltpu.VMEM((4, rows // 4, width), texts.dtype),
            pltpu.SemaphoreType.DMA((8,)),
        ],
        compiler_params=params(58),
        cost_estimate=COST,
    )(texts)


def cut_rows(half):
    return [half // 2, half // 2]


def pairs(scalars_ref, texts, images, pieces, weights, low, tile, own=False, arrive=None, leave=None, bases=None):
    scale, bias = scalars_ref[0], scalars_ref[1]
    rate, offset = -LOG2_E * scale, -LOG2_E * bias
    tiles = [(k, start) for k, text in enumerate(texts) for start in range(0, text.shape[0], tile)]
    places = [(piece, start) for piece in pieces for start in range(0, piece.shape[0], tile)]

    def low_rows(i):
        k, start = tiles[i]
        base = i * tile if bases is None else bases[k] + start
        return slice(base, base + tile)

    def exponents(i):
        k, start = tiles[i]
        if start == 0 and arrive is not None:
            arrive(k)
        unit, _ = unit_rows(texts[k][start : start + tile, :])
        unit = unit.astype(jnp.bfloat16)
        low[low_rows(i), :] = unit
        return rate * dot(unit, images(k), 1, 1) + offset

    ahead = exponents(0)
    for i, (k, start) in enumerate(tiles):
        exponent = ahead
        if i + 1 < len(tiles):
            ahead = exponents(i + 1)
        if own:
            row = i * tile + lax.broadcasted_iota(jnp.int32, exponent.shape, 0)
            column = lax.broadcasted_iota(jnp.int32, exponent.shape, 1)
            sign = jnp.where(row == column, -1.0, 1.0)
            weight = (sign / (1.0 + jnp.exp2(sign * exponent))).astype(jnp.bfloat16)
        else:
            weight = (1.0 / (1.0 + jnp.exp2(exponent))).astype(jnp.bfloat16)
        weights[low_rows(i), :] = weight
        product = scale * dot(weight, images(k), 1, 0)
        piece, place = places[i]
        piece[place : place + tile, :] = product.astype(piece.dtype)
        if leave is not None and start + tile == texts[k].shape[0]:
            leave(k)


def own_kernel(tile, scalars_ref, texts_ref, raw_ref, images_ref, partial_ref, sum_ref, *scratch):
    texts, raw, images, low, weights, sems = scratch
    copy = lambda source, target, k: pltpu.make_async_copy(source, target, sems.at[k])
    load_raw, load_texts = copy(raw_ref, raw, 0), copy(texts_ref, texts, 1)
    load_raw.start()
    load_texts.start()
    load_raw.wait()
    store_unit_rows(raw, images, tile)
    store_images = copy(images, images_ref, 0)
    store_images.start()
    load_texts.wait()
    pairs(
        scalars_ref, [texts], lambda k: images[...], [partial_ref], weights, low, tile, own=True
    )

    @pl.loop(0, sum_ref.shape[0] // tile)
    def _(i):
        here = pl.ds(pl.multiple_of(i * tile, tile), tile)
        sum_ref[here, :] = scalars_ref[0] * dot(weights[:, here], low[...], 0, 0)

    store_images.wait()


def own_pair(scalars, texts, raw, tile=256):
    rows, width = raw.shape
    return pl.pallas_call(
        functools.partial(own_kernel, tile),
        out_shape=[
            like(rows, width, jnp.bfloat16),
            like(rows, width, jnp.float32),
            like(rows, width, jnp.float32),
        ],
        in_specs=[IN_SMEM, IN_HBM, IN_HBM],
        out_specs=[IN_HBM, IN_VMEM, IN_VMEM],
        scratch_shapes=[pltpu.VMEM((rows, width), jnp.bfloat16)] * 4
        + [pltpu.VMEM((rows, rows), jnp.bfloat16), pltpu.SemaphoreType.DMA((2,))],
        compiler_params=params(58),
        cost_estimate=COST,
    )(scalars, texts, raw)


def near_kernel(tile, slots_ref, scalars_ref, own_ref, raw_ref, *refs):
    count = (len(refs) - 10) // 2
    sources, outs = refs[:count], refs[count : 2 * count]
    images_ref, weights_ref, low_ref, images, raw, texts, pieces, weights, low, sems = refs[
        2 * count :
    ]
    half = sources[0].shape[0]
    copy = lambda source, target, k: pltpu.make_async_copy(source, target, sems.at[k])
    load_own = copy(own_ref, images.at[0], 1)
    loads = [copy(source, texts.at[k], 2 + k) for k, source in enumerate(sources)]
    load_raw = copy(raw_ref, raw, 0)
    for load in (load_raw, load_own, loads[0]):
        load.start()
    load_raw.wait()
    for load in loads[1:]:
        load.start()
    store_unit_rows(raw, images.at[1], tile)
    store_images = copy(images.at[1], images_ref, 0)
    store_images.start()
    load_own.wait()
    stores = []

    def leave(k):
        rows = pl.ds(k * half, half)
        first = 2 + count + 3 * k
        stores.append(copy(pieces.at[k], outs[k], first))
        stores.append(copy(weights.at[rows], weights_ref.at[rows], first + 1))
        stores.append(copy(low.at[rows], low_ref.at[rows], first + 2))
        for store in stores[-3:]:
            store.start()

    pairs(
        scalars_ref,
        [texts.at[k] for k in range(count)],
        lambda k: images[slots_ref[k]],
        [pieces.at[k] for k in range(count)],
        weights,
        low,
        tile,
        arrive=lambda k: loads[k].wait(),
        leave=leave,
    )
    for store in (store_images, *stores):
        store.wait()


def near_pairs(slots, scalars, own_images, raw, texts, tile=256):
    rows, width = raw.shape
    half, count = texts[0].shape[0], len(texts)
    bf16 = jnp.bfloat16
    return pl.pallas_call(
        functools.partial(near_kernel, tile),
        out_shape=[like(half, width, bf16)] * count
        + [like(rows, width, bf16), like(count * half, rows, bf16), like(count * half, width, bf16)],
        in_specs=[IN_SMEM, IN_SMEM] + [IN_HBM] * (2 + count),
        out_specs=[IN_HBM] * (count + 3),
        scratch_shapes=[
            pltpu.VMEM((2, rows, width), bf16),
            pltpu.VMEM((rows, width), bf16),
            pltpu.VMEM((count, half, width), bf16),
            pltpu.VMEM((count, half, width), bf16),
            pltpu.VMEM((count * half, rows), bf16),
            pltpu.VMEM((count * half, width), bf16),
            pltpu.SemaphoreType.DMA((2 + 4 * count,)),
        ],
        compiler_params=params(58),
        cost_estimate=COST,
    )(slots, scalars, own_images, raw, *texts)


def pair_sums_kernel(tile, slots_ref, scalars_ref, own_ref, next_ref, sum_ref, *refs):
    weights_ref, low_ref = refs[:2]
    sources, outs = refs[2:4], refs[4:8]
    sums_ref, images, texts, pieces, weights, low, sums, sems = refs[8:]
    half = sources[0].shape[0]
    scale = scalars_ref[0]
    copy = lambda source, target, k: pltpu.make_async_copy(source, target, sems.at[k])
    load_images = [copy(own_ref, images.at[k], k) for k in range(2)]
    load_next = [copy(next_ref, images.at[k], k) for k in range(2)]
    load_texts = [copy(ref, texts.at[k], 2 + k) for k, ref in enumerate(sources)]

    def start_images(k):
        pl.when(slots_ref[1 - k] == 0)(load_images[k].start)
        pl.when(slots_ref[1 - k] != 0)(load_next[k].start)

    spans = [pl.ds(k * half, half) for k in range(4)]
    load_rest = [copy(sum_ref, sums.at[0], 4)]
    for k, (source, target) in enumerate(((0, 3), (1, 1))):
        load_rest.append(copy(weights_ref.at[spans[source]], weights.at[spans[target]], 5 + 2 * k))
        load_rest.append(copy(low_ref.at[spans[source]], low.at[spans[target]], 6 + 2 * k))
    start_images(0)
    load_texts[0].start()
    sums[1] = jnp.zeros(sums.shape[1:], jnp.float32)
    load_images[0].wait()
    start_images(1)
    for load in (load_texts[1], *load_rest):
        load.start()

    def arrive(k):
        load_texts[k].wait()
        if k == 1:
            load_images[1].wait()

    cuts = [
        copy(pieces.at[i // 2, pl.ds(i % 2 * outs[0].shape[0], out.shape[0])], out, 9 + i)
        for i, out in enumerate(outs)
    ]

    def leave(k):
        for cut in cuts[2 * k : 2 * k + 2]:
            cut.start()

    pairs(
        scalars_ref,
        [texts.at[k] for k in range(2)],
        lambda k: images[k],
        [pieces.at[k] for k in range(2)],
        weights,
        low,
        tile,
        arrive=arrive,
        leave=leave,
        bases=(0, 2 * half),
    )
    for load in load_rest:
        load.wait()
    count = sums.shape[1] // tile

    def store(i):
        part = pl.ds(pl.multiple_of(i * tile, tile), tile)
        return copy(sums.at[:, part], sums_ref.at[:, part], i)

    @pl.loop(0, count)
    def _(i):
        part = pl.ds(pl.multiple_of(i * tile, tile), tile)
        for k in range(2):
            rows = slice(2 * k * half, 2 * (k + 1) * half)
            sums[slots_ref[1 - k], part, :] += scale * dot(weights[rows, part], low[rows, :], 0, 0)
        store(i).start()

    for i in range(count):
        store(i).wait()
    for cut in cuts:
        cut.wait()


def pair_sums(slots, scalars, own_images, next_images, own, weights, low, texts, tile=256):
    rows, width = own.shape
    half = texts[0].shape[0]
    bf16 = jnp.bfloat16
    return pl.pallas_call(
        functools.partial(pair_sums_kernel, tile),
        out_shape=[like(size, width, bf16) for size in cut_rows(half) * 2]
        + [jax.ShapeDtypeStruct((2, rows, width), jnp.float32)],
        in_specs=[IN_SMEM, IN_SMEM] + [IN_HBM] * 7,
        out_specs=[IN_HBM] * 5,
        scratch_shapes=[
            pltpu.VMEM((2, rows, width), bf16),
            pltpu.VMEM((2, half, width), bf16),
            pltpu.VMEM((2, half, width), bf16),
            pltpu.VMEM((4 * half, rows), bf16),
            pltpu.VMEM((4 * half, width), bf16),
            pltpu.VMEM((2, rows, width), jnp.float32),
            pltpu.SemaphoreType.DMA((13,)),
        ],
        compiler_params=params(58),
        cost_estimate=COST,
    )(slots, scalars, own_images, next_images, own, weights, low, *texts)


def far_kernel(tile, slot_ref, scalars_ref, own_ref, next_ref, sums_ref, *refs):
    sources, outs = refs[:2], refs[2:6]
    total_ref, ready_ref, images, texts, pieces, weights, low, sums, ready, sems = refs[6:]
    half = sources[0].shape[0]
    copy = lambda source, target, k: pltpu.make_async_copy(source, target, sems.at[k])
    load_own, load_next = copy(own_ref, images, 0), copy(next_ref, images, 0)
    loads = [copy(source, texts.at[k], 1 + k) for k, source in enumerate(sources)]
    load_sums = copy(sums_ref, sums, 3)
    pl.when(slot_ref[0] == 0)(load_own.start)
    pl.when(slot_ref[0] != 0)(load_next.start)
    loads[0].start()
    load_own.wait()
    loads[1].start()
    load_sums.start()
    cuts = [
        copy(pieces.at[i // 2, pl.ds(i % 2 * outs[0].shape[0], out.shape[0])], out, 8 + i)
        for i, out in enumerate(outs)
    ]

    def leave(k):
        for cut in cuts[2 * k : 2 * k + 2]:
            cut.start()

    pairs(
        scalars_ref,
        [texts.at[k] for k in range(2)],
        lambda k: images[...],
        [pieces.at[k] for k in range(2)],
        weights,
        low,
        tile,
        arrive=lambda k: loads[k].wait(),
        leave=leave,
    )
    load_sums.wait()
    next_share = scalars_ref[0] * slot_ref[0].astype(jnp.float32)
    own_share = scalars_ref[0] - next_share
    count = sums.shape[1] // tile

    def stores(i):
        part = pl.ds(pl.multiple_of(i * tile, tile), tile)
        return (
            copy(ready.at[part], ready_ref.at[part], 4 + i),
            copy(sums.at[0, part], total_ref.at[part], i),
        )

    @pl.loop(0, count)
    def _(i):
        part = pl.ds(pl.multiple_of(i * tile, tile), tile)
        product = dot(weights[:, part], low[...], 0, 0)
        ready[part, :] = (sums[1, part, :] + next_share * product).astype(ready.dtype)
        sums[0, part, :] += own_share * product
        for store in stores(i):
            store.start()

    for i in range(count):
        for store in stores(i):
            store.wait()
    for cut in cuts:
        cut.wait()


def far_pair(slot, scalars, own_images, next_images, sums, texts, tile=256):
    rows, width = own_images.shape
    half = texts[0].shape[0]
    bf16 = jnp.bfloat16
    return pl.pallas_call(
        functools.partial(far_kernel, tile),
        out_shape=[like(size, width, bf16) for size in cut_rows(half) * 2]
        + [like(rows, width, jnp.float32), like(rows, width, bf16)],
        in_specs=[IN_SMEM, IN_SMEM] + [IN_HBM] * 5,
        out_specs=[IN_HBM] * 6,
        scratch_shapes=[
            pltpu.VMEM((rows, width), bf16),
            pltpu.VMEM((2, half, width), bf16),
            pltpu.VMEM((2, half, width), bf16),
            pltpu.VMEM((2 * half, rows), bf16),
            pltpu.VMEM((2 * half, width), bf16),
            pltpu.VMEM((2, rows, width), jnp.float32),
            pltpu.VMEM((rows, width), bf16),
            pltpu.SemaphoreType.DMA((12,)),
        ],
        compiler_params=params(58),
        cost_estimate=COST,
    )(slot, scalars, own_images, next_images, sums, *texts)


def finish_rows(raw, direction):
    unit, inverse = unit_rows(raw)
    inner = jnp.sum(unit * direction, axis=-1, keepdims=True)
    return inverse * (direction - unit * inner)


def finish_images_kernel(raw_ref, own_ref, back_ref, grad_ref):
    direction = own_ref[...] + back_ref[...].astype(jnp.float32)
    grad_ref[...] = finish_rows(raw_ref[...], direction)


def finish_images(raw, own, back):
    rows, width = raw.shape
    tile = rows // 2
    flat = pl.BlockSpec((tile, width), lambda i: (i, 0))
    return pl.pallas_call(
        finish_images_kernel,
        grid=(rows // tile,),
        out_shape=jax.ShapeDtypeStruct((rows, width), jnp.float32),
        in_specs=[flat] * 3,
        out_specs=flat,
        compiler_params=params(14),
        cost_estimate=COST,
    )(raw, own, back)


def first_texts_kernel(raw_ref, own_ref, *refs):
    near_refs, last_refs, grad_ref = refs[:2], refs[2:4], refs[4]
    rows = raw_ref.shape[0]
    for half in range(2):

        @pl.when(pl.program_id(0) == half)
        def _():
            direction = own_ref[...] + near_refs[half][:rows, :].astype(jnp.float32)
            direction = direction + last_refs[half][...].astype(jnp.float32)
            grad_ref[...] = finish_rows(raw_ref[...], direction)


def finish_first_texts(raw, own, near, last):
    rows, width = raw.shape
    flat = pl.BlockSpec((rows // 4, width), lambda i: (2 * i, 0))
    return pl.pallas_call(
        first_texts_kernel,
        grid=(2,),
        out_shape=like(rows, width, jnp.float32),
        in_specs=[flat] * 2 + [IN_VMEM] * 4,
        out_specs=flat,
        compiler_params=params(14),
        cost_estimate=COST,
    )(raw, own, *near, *last)


def gather_kernel(raw_ref, own_ref, *refs):
    near_refs, (rows_ref, base_ref) = refs[:2], refs[2:]
    rows = raw_ref.shape[0]
    rows_ref[...] = raw_ref[...]
    for half in range(2):

        @pl.when(pl.program_id(0) == half)
        def _():
            base_ref[...] = own_ref[...] + near_refs[half][rows:, :].astype(jnp.float32)


def gather_last_texts(raw, own, near):
    rows, width = raw.shape
    flat = pl.BlockSpec((rows // 4, width), lambda i: (2 * i + 1, 0))
    out = pl.BlockSpec((rows // 4, width), lambda i: (i, 0))
    return pl.pallas_call(
        gather_kernel,
        grid=(2,),
        out_shape=[like(rows // 2, width, raw.dtype), like(rows // 2, width, jnp.float32)],
        in_specs=[flat] * 2 + [IN_VMEM] * 2,
        out_specs=[out] * 2,
        compiler_params=params(14),
        cost_estimate=COST,
    )(raw, own, *near)


def last_texts_kernel(raw_ref, base_ref, *refs):
    last_refs, grad_ref = refs[:2], refs[-1]
    rows = grad_ref.shape[0]
    for half in range(2):

        @pl.when(pl.program_id(0) == half)
        def _():
            here = slice(half * rows, (half + 1) * rows)
            direction = base_ref[here, :] + last_refs[half][...].astype(jnp.float32)
            grad_ref[...] = finish_rows(raw_ref[here, :], direction)


def finish_last_texts(raw, base, last, held):
    rows, width = held.shape
    return pl.pallas_call(
        last_texts_kernel,
        grid=(2,),
        out_shape=like(rows, width, jnp.float32),
        in_specs=[IN_VMEM] * 4 + [pl.BlockSpec(memory_space=pl.ANY)],
        out_specs=pl.BlockSpec((rows // 4, width), lambda i: (2 * i + 1, 0)),
        input_output_aliases={4: 0},
        compiler_params=params(14),
        cost_estimate=COST,
    )(raw, base, *last, held)


def body(images_raw, texts_raw, inverse_softness, additive_shift_term):
    count = lax.axis_size("wide") * lax.axis_size("narrow")
    z = lax.axis_index("narrow") % RING
    scalars = jnp.concatenate([inverse_softness, additive_shift_term])
    slot = [jnp.where(z < RING - t, 1, 0).astype(jnp.int32).reshape(1) for t in range(RING)]
    slots = lambda *places: jnp.concatenate([slot[t] for t in places])
    up, down = ring_route(1, count), ring_route(-1, count)

    images_next_raw = send(images_raw, line_route(-RING, count))
    own_a, own_b = halves(texts_raw)
    left_a = send(own_a, up)
    right_b = send(own_b, down)
    images, text_own, own_sum = own_pair(scalars, texts_raw, images_raw)
    left_b = send(after(own_b, own_sum), up)
    right_a = send(after(own_a, own_sum), down)
    far_a = send(left_a, up)
    far_b = send(right_b, down)

    near_slots = slots(3, 1)
    left_part_a, right_part_b, images_next, weights, low = near_pairs(
        near_slots, scalars, images, images_next_raw, [left_a, right_b]
    )
    from_right_a = send(left_part_a, down)
    from_left_b = send(right_part_b, up)
    right_a1, right_a2, left_b1, left_b2, sums = pair_sums(
        near_slots, scalars, images, images_next, own_sum, weights, low, [right_a, left_b]
    )
    *far_parts, own_sum, next_sum = far_pair(
        slots(2), scalars, images, images_next, sums, [far_a, far_b]
    )
    far_a1, far_b1 = send(far_parts[0], up), send(far_parts[2], down)
    images_back = send(next_sum, line_route(RING, count))
    near = (from_right_a, from_left_b)
    far_a2 = send(after(far_parts[1], next_sum, *near), up)
    far_b2 = send(after(far_parts[3], next_sum, *near), down)

    rows_last, base_last = gather_last_texts(texts_raw, text_own, near)

    def relay(part, far, route):
        total = after(part, own_sum, base_last).astype(jnp.float32) + far.astype(jnp.float32)
        return send(total.astype(jnp.bfloat16), route)

    from_left_a1 = relay(right_a1, far_a1, up)
    from_right_b1 = relay(left_b1, far_b1, down)
    from_left_a2 = relay(right_a2, far_a2, up)
    from_right_b2 = relay(left_b2, far_b2, down)
    image_grad = finish_images(images_raw, own_sum, images_back)
    text_grad = finish_first_texts(texts_raw, text_own, near, (from_left_a1, from_right_b1))
    text_grad = finish_last_texts(
        rows_last, after(base_last, image_grad), (from_left_a2, from_right_b2), text_grad
    )
    return image_grad, text_grad


def solution(mesh):
    spec = P(AXES, None)
    return jax.shard_map(
        body,
        mesh=mesh,
        in_specs=(spec, spec, P(), P()),
        out_specs=(spec, spec),
        check_vma=False,
    )
```

```python
import functools

import jax
import jax.numpy as jnp
from jax import lax
from jax.experimental import pallas as pl
from jax.experimental.pallas import tpu as pltpu
from jax.sharding import PartitionSpec as P

AXES = ("wide", "narrow")
RING = 4
LOG2_E = 1.4426950408889634
MIB = 1024 * 1024
COST = pl.CostEstimate(flops=1000, bytes_accessed=1000, transcendentals=0)
IN_SMEM = pl.BlockSpec(memory_space=pltpu.SMEM)
IN_VMEM = pl.BlockSpec(memory_space=pltpu.VMEM)
IN_HBM = pl.BlockSpec(memory_space=pltpu.HBM)


def ring_route(step, count):
    return [(d, d - d % RING + (d + step) % RING) for d in range(count)]


def line_route(step, count):
    return [(d, (d + step) % count) for d in range(count)]


def send(block, route):
    return lax.ppermute(block, AXES, route)


def after(value, *earlier):
    return lax.optimization_barrier((value, *earlier))[0]


def params(mib):
    return pltpu.CompilerParams(vmem_limit_bytes=mib * MIB)


def like(rows, width, dtype):
    return jax.ShapeDtypeStruct((rows, width), dtype)


def dot(left, right, left_dim, right_dim):
    contract = (((left_dim,), (right_dim,)), ((), ()))
    return lax.dot_general(left, right, contract, preferred_element_type=jnp.float32)


def unit_rows(raw):
    wide = raw.astype(jnp.float32)
    inverse = lax.rsqrt(jnp.sum(wide * wide, axis=-1, keepdims=True) + 1e-06)
    return wide * inverse, inverse


def store_unit_rows(raw_ref, unit_ref, tile):
    for start in range(0, raw_ref.shape[0], tile):
        unit, _ = unit_rows(raw_ref[start : start + tile, :])
        unit_ref[start : start + tile, :] = unit.astype(unit_ref.dtype)


def halves_kernel(texts_ref, first_ref, second_ref, chunks, sems):
    count, rows = chunks.shape[:2]
    loads = [
        pltpu.make_async_copy(texts_ref.at[pl.ds(k * rows, rows)], chunks.at[k], sems.at[k])
        for k in range(count)
    ]
    stores = []
    for k in range(count):
        out = first_ref if 2 * k < count else second_ref
        place = out.at[pl.ds(k % (count // 2) * rows, rows)]
        stores.append(pltpu.make_async_copy(chunks.at[k], place, sems.at[count + k]))
    for load in loads:
        load.start()
    for load, store in zip(loads, stores):
        load.wait()
        store.start()
    for store in stores:
        store.wait()


def halves(texts):
    rows, width = texts.shape
    return pl.pallas_call(
        halves_kernel,
        out_shape=[like(rows // 2, width, texts.dtype)] * 2,
        in_specs=[IN_HBM],
        out_specs=[IN_HBM] * 2,
        scratch_shapes=[
            pltpu.VMEM((4, rows // 4, width), texts.dtype),
            pltpu.SemaphoreType.DMA((8,)),
        ],
        compiler_params=params(58),
        cost_estimate=COST,
    )(texts)


def cut_rows(half):
    return [half // 2, half // 2]


def pairs(scalars_ref, texts, images, pieces, weights, low, tile, own=False, arrive=None, leave=None, bases=None):
    scale, bias = scalars_ref[0], scalars_ref[1]
    rate, offset = -LOG2_E * scale, -LOG2_E * bias
    tiles = [(k, start) for k, text in enumerate(texts) for start in range(0, text.shape[0], tile)]
    places = [(piece, start) for piece in pieces for start in range(0, piece.shape[0], tile)]

    def low_rows(i):
        k, start = tiles[i]
        base = i * tile if bases is None else bases[k] + start
        return slice(base, base + tile)

    def exponents(i):
        k, start = tiles[i]
        if start == 0 and arrive is not None:
            arrive(k)
        unit, _ = unit_rows(texts[k][start : start + tile, :])
        unit = unit.astype(jnp.bfloat16)
        low[low_rows(i), :] = unit
        return rate * dot(unit, images(k), 1, 1) + offset

    ahead = exponents(0)
    for i, (k, start) in enumerate(tiles):
        exponent = ahead
        if i + 1 < len(tiles):
            ahead = exponents(i + 1)
        if own:
            row = i * tile + lax.broadcasted_iota(jnp.int32, exponent.shape, 0)
            column = lax.broadcasted_iota(jnp.int32, exponent.shape, 1)
            sign = jnp.where(row == column, -1.0, 1.0)
            weight = (sign / (1.0 + jnp.exp2(sign * exponent))).astype(jnp.bfloat16)
        else:
            weight = (1.0 / (1.0 + jnp.exp2(exponent))).astype(jnp.bfloat16)
        weights[low_rows(i), :] = weight
        product = scale * dot(weight, images(k), 1, 0)
        piece, place = places[i]
        piece[place : place + tile, :] = product.astype(piece.dtype)
        if leave is not None and start + tile == texts[k].shape[0]:
            leave(k)


def own_kernel(tile, scalars_ref, texts_ref, raw_ref, images_ref, partial_ref, sum_ref, *scratch):
    texts, raw, images, low, weights, sems = scratch
    copy = lambda source, target, k: pltpu.make_async_copy(source, target, sems.at[k])
    load_raw, load_texts = copy(raw_ref, raw, 0), copy(texts_ref, texts, 1)
    load_raw.start()
    load_texts.start()
    load_raw.wait()
    store_unit_rows(raw, images, tile)
    store_images = copy(images, images_ref, 0)
    store_images.start()
    load_texts.wait()
    pairs(
        scalars_ref, [texts], lambda k: images[...], [partial_ref], weights, low, tile, own=True
    )

    @pl.loop(0, sum_ref.shape[0] // tile)
    def _(i):
        here = pl.ds(pl.multiple_of(i * tile, tile), tile)
        sum_ref[here, :] = scalars_ref[0] * dot(weights[:, here], low[...], 0, 0)

    store_images.wait()


def own_pair(scalars, texts, raw, tile=256):
    rows, width = raw.shape
    return pl.pallas_call(
        functools.partial(own_kernel, tile),
        out_shape=[
            like(rows, width, jnp.bfloat16),
            like(rows, width, jnp.float32),
            like(rows, width, jnp.float32),
        ],
        in_specs=[IN_SMEM, IN_HBM, IN_HBM],
        out_specs=[IN_HBM, IN_VMEM, IN_VMEM],
        scratch_shapes=[pltpu.VMEM((rows, width), jnp.bfloat16)] * 4
        + [pltpu.VMEM((rows, rows), jnp.bfloat16), pltpu.SemaphoreType.DMA((2,))],
        compiler_params=params(58),
        cost_estimate=COST,
    )(scalars, texts, raw)


def near_kernel(tile, slots_ref, scalars_ref, own_ref, raw_ref, *refs):
    count = (len(refs) - 10) // 2
    sources, outs = refs[:count], refs[count : 2 * count]
    images_ref, weights_ref, low_ref, images, raw, texts, pieces, weights, low, sems = refs[
        2 * count :
    ]
    half = sources[0].shape[0]
    copy = lambda source, target, k: pltpu.make_async_copy(source, target, sems.at[k])
    load_own = copy(own_ref, images.at[0], 1)
    loads = [copy(source, texts.at[k], 2 + k) for k, source in enumerate(sources)]
    parts = [pl.ds(k * half, half) for k in range(2)]
    load_raw = [
        copy(raw_ref.at[part], raw.at[part], k)
        for part, k in zip(parts, (0, 2 + 4 * count))
    ]
    for load in (*load_raw, load_own, loads[0]):
        load.start()
    for load, part in zip(load_raw, parts):
        load.wait()
        store_unit_rows(raw.at[part], images.at[1, part], tile)
    for load in loads[1:]:
        load.start()
    store_images = copy(images.at[1], images_ref, 0)
    store_images.start()
    load_own.wait()
    stores = []

    def leave(k):
        rows = pl.ds(k * half, half)
        first = 2 + count + 3 * k
        stores.append(copy(pieces.at[k], outs[k], first))
        stores.append(copy(weights.at[rows], weights_ref.at[rows], first + 1))
        stores.append(copy(low.at[rows], low_ref.at[rows], first + 2))
        for store in stores[-3:]:
            store.start()

    pairs(
        scalars_ref,
        [texts.at[k] for k in range(count)],
        lambda k: images[slots_ref[k]],
        [pieces.at[k] for k in range(count)],
        weights,
        low,
        tile,
        arrive=lambda k: loads[k].wait(),
        leave=leave,
    )
    for store in (store_images, *stores):
        store.wait()


def near_pairs(slots, scalars, own_images, raw, texts, tile=256):
    rows, width = raw.shape
    half, count = texts[0].shape[0], len(texts)
    bf16 = jnp.bfloat16
    return pl.pallas_call(
        functools.partial(near_kernel, tile),
        out_shape=[like(half, width, bf16)] * count
        + [like(rows, width, bf16), like(count * half, rows, bf16), like(count * half, width, bf16)],
        in_specs=[IN_SMEM, IN_SMEM] + [IN_HBM] * (2 + count),
        out_specs=[IN_HBM] * (count + 3),
        scratch_shapes=[
            pltpu.VMEM((2, rows, width), bf16),
            pltpu.VMEM((rows, width), bf16),
            pltpu.VMEM((count, half, width), bf16),
            pltpu.VMEM((count, half, width), bf16),
            pltpu.VMEM((count * half, rows), bf16),
            pltpu.VMEM((count * half, width), bf16),
            pltpu.SemaphoreType.DMA((3 + 4 * count,)),
        ],
        compiler_params=params(58),
        cost_estimate=COST,
    )(slots, scalars, own_images, raw, *texts)


def pair_sums_kernel(tile, slots_ref, scalars_ref, own_ref, next_ref, sum_ref, *refs):
    weights_ref, low_ref = refs[:2]
    sources, outs = refs[2:4], refs[4:8]
    sums_ref, images, texts, pieces, weights, low, sums, sems = refs[8:]
    half = sources[0].shape[0]
    scale = scalars_ref[0]
    copy = lambda source, target, k: pltpu.make_async_copy(source, target, sems.at[k])
    load_images = [copy(own_ref, images.at[k], k) for k in range(2)]
    load_next = [copy(next_ref, images.at[k], k) for k in range(2)]
    load_texts = [copy(ref, texts.at[k], 2 + k) for k, ref in enumerate(sources)]

    def start_images(k):
        pl.when(slots_ref[1 - k] == 0)(load_images[k].start)
        pl.when(slots_ref[1 - k] != 0)(load_next[k].start)

    spans = [pl.ds(k * half, half) for k in range(4)]
    load_rest = [copy(sum_ref, sums.at[0], 4)]
    for k, (source, target) in enumerate(((0, 3), (1, 1))):
        load_rest.append(copy(weights_ref.at[spans[source]], weights.at[spans[target]], 5 + 2 * k))
        load_rest.append(copy(low_ref.at[spans[source]], low.at[spans[target]], 6 + 2 * k))
    start_images(0)
    load_texts[0].start()
    sums[1] = jnp.zeros(sums.shape[1:], jnp.float32)
    load_images[0].wait()
    start_images(1)
    for load in (load_texts[1], *load_rest):
        load.start()

    def arrive(k):
        load_texts[k].wait()
        if k == 1:
            load_images[1].wait()

    cuts = [
        copy(pieces.at[i // 2, pl.ds(i % 2 * outs[0].shape[0], out.shape[0])], out, 9 + i)
        for i, out in enumerate(outs)
    ]

    def leave(k):
        for cut in cuts[2 * k : 2 * k + 2]:
            cut.start()

    pairs(
        scalars_ref,
        [texts.at[k] for k in range(2)],
        lambda k: images[k],
        [pieces.at[k] for k in range(2)],
        weights,
        low,
        tile,
        arrive=arrive,
        leave=leave,
        bases=(0, 2 * half),
    )
    for load in load_rest:
        load.wait()
    count = sums.shape[1] // tile

    def store(i):
        part = pl.ds(pl.multiple_of(i * tile, tile), tile)
        return copy(sums.at[:, part], sums_ref.at[:, part], i)

    @pl.loop(0, count)
    def _(i):
        part = pl.ds(pl.multiple_of(i * tile, tile), tile)
        for k in range(2):
            rows = slice(2 * k * half, 2 * (k + 1) * half)
            sums[slots_ref[1 - k], part, :] += scale * dot(weights[rows, part], low[rows, :], 0, 0)
        store(i).start()

    for i in range(count):
        store(i).wait()
    for cut in cuts:
        cut.wait()


def pair_sums(slots, scalars, own_images, next_images, own, weights, low, texts, tile=256):
    rows, width = own.shape
    half = texts[0].shape[0]
    bf16 = jnp.bfloat16
    return pl.pallas_call(
        functools.partial(pair_sums_kernel, tile),
        out_shape=[like(size, width, bf16) for size in cut_rows(half) * 2]
        + [jax.ShapeDtypeStruct((2, rows, width), jnp.float32)],
        in_specs=[IN_SMEM, IN_SMEM] + [IN_HBM] * 7,
        out_specs=[IN_HBM] * 5,
        scratch_shapes=[
            pltpu.VMEM((2, rows, width), bf16),
            pltpu.VMEM((2, half, width), bf16),
            pltpu.VMEM((2, half, width), bf16),
            pltpu.VMEM((4 * half, rows), bf16),
            pltpu.VMEM((4 * half, width), bf16),
            pltpu.VMEM((2, rows, width), jnp.float32),
            pltpu.SemaphoreType.DMA((13,)),
        ],
        compiler_params=params(58),
        cost_estimate=COST,
    )(slots, scalars, own_images, next_images, own, weights, low, *texts)


def far_kernel(tile, slot_ref, scalars_ref, own_ref, next_ref, sums_ref, *refs):
    sources, outs = refs[:2], refs[2:6]
    total_ref, ready_ref, images, texts, pieces, weights, low, sums, ready, sems = refs[6:]
    half = sources[0].shape[0]
    copy = lambda source, target, k: pltpu.make_async_copy(source, target, sems.at[k])
    load_own, load_next = copy(own_ref, images, 0), copy(next_ref, images, 0)
    loads = [copy(source, texts.at[k], 1 + k) for k, source in enumerate(sources)]
    load_sums = copy(sums_ref, sums, 3)
    pl.when(slot_ref[0] == 0)(load_own.start)
    pl.when(slot_ref[0] != 0)(load_next.start)
    loads[0].start()
    load_own.wait()
    loads[1].start()
    load_sums.start()
    cuts = [
        copy(pieces.at[i // 2, pl.ds(i % 2 * outs[0].shape[0], out.shape[0])], out, 8 + i)
        for i, out in enumerate(outs)
    ]

    def leave(k):
        for cut in cuts[2 * k : 2 * k + 2]:
            cut.start()

    pairs(
        scalars_ref,
        [texts.at[k] for k in range(2)],
        lambda k: images[...],
        [pieces.at[k] for k in range(2)],
        weights,
        low,
        tile,
        arrive=lambda k: loads[k].wait(),
        leave=leave,
    )
    load_sums.wait()
    next_share = scalars_ref[0] * slot_ref[0].astype(jnp.float32)
    own_share = scalars_ref[0] - next_share
    count = sums.shape[1] // tile

    def stores(i):
        part = pl.ds(pl.multiple_of(i * tile, tile), tile)
        return (
            copy(ready.at[part], ready_ref.at[part], 4 + i),
            copy(sums.at[0, part], total_ref.at[part], i),
        )

    @pl.loop(0, count)
    def _(i):
        part = pl.ds(pl.multiple_of(i * tile, tile), tile)
        product = dot(weights[:, part], low[...], 0, 0)
        ready[part, :] = (sums[1, part, :] + next_share * product).astype(ready.dtype)
        sums[0, part, :] += own_share * product
        for store in stores(i):
            store.start()

    for i in range(count):
        for store in stores(i):
            store.wait()
    for cut in cuts:
        cut.wait()


def far_pair(slot, scalars, own_images, next_images, sums, texts, tile=256):
    rows, width = own_images.shape
    half = texts[0].shape[0]
    bf16 = jnp.bfloat16
    return pl.pallas_call(
        functools.partial(far_kernel, tile),
        out_shape=[like(size, width, bf16) for size in cut_rows(half) * 2]
        + [like(rows, width, jnp.float32), like(rows, width, bf16)],
        in_specs=[IN_SMEM, IN_SMEM] + [IN_HBM] * 5,
        out_specs=[IN_HBM] * 6,
        scratch_shapes=[
            pltpu.VMEM((rows, width), bf16),
            pltpu.VMEM((2, half, width), bf16),
            pltpu.VMEM((2, half, width), bf16),
            pltpu.VMEM((2 * half, rows), bf16),
            pltpu.VMEM((2 * half, width), bf16),
            pltpu.VMEM((2, rows, width), jnp.float32),
            pltpu.VMEM((rows, width), bf16),
            pltpu.SemaphoreType.DMA((12,)),
        ],
        compiler_params=params(58),
        cost_estimate=COST,
    )(slot, scalars, own_images, next_images, sums, *texts)


def finish_rows(raw, direction):
    unit, inverse = unit_rows(raw)
    inner = jnp.sum(unit * direction, axis=-1, keepdims=True)
    return inverse * (direction - unit * inner)


def finish_images_kernel(raw_ref, own_ref, back_ref, grad_ref):
    direction = own_ref[...] + back_ref[...].astype(jnp.float32)
    grad_ref[...] = finish_rows(raw_ref[...], direction)


def finish_images(raw, own, back):
    rows, width = raw.shape
    tile = rows // 2
    flat = pl.BlockSpec((tile, width), lambda i: (i, 0))
    return pl.pallas_call(
        finish_images_kernel,
        grid=(rows // tile,),
        out_shape=jax.ShapeDtypeStruct((rows, width), jnp.float32),
        in_specs=[flat] * 3,
        out_specs=flat,
        compiler_params=params(14),
        cost_estimate=COST,
    )(raw, own, back)


def first_texts_kernel(raw_ref, own_ref, *refs):
    near_refs, last_refs, grad_ref = refs[:2], refs[2:4], refs[4]
    rows = raw_ref.shape[0]
    for half in range(2):

        @pl.when(pl.program_id(0) == half)
        def _():
            direction = own_ref[...] + near_refs[half][:rows, :].astype(jnp.float32)
            direction = direction + last_refs[half][...].astype(jnp.float32)
            grad_ref[...] = finish_rows(raw_ref[...], direction)


def finish_first_texts(raw, own, near, last):
    rows, width = raw.shape
    flat = pl.BlockSpec((rows // 4, width), lambda i: (2 * i, 0))
    return pl.pallas_call(
        first_texts_kernel,
        grid=(2,),
        out_shape=like(rows, width, jnp.float32),
        in_specs=[flat] * 2 + [IN_VMEM] * 4,
        out_specs=flat,
        compiler_params=params(14),
        cost_estimate=COST,
    )(raw, own, *near, *last)


def gather_kernel(raw_ref, own_ref, *refs):
    near_refs, (rows_ref, base_ref) = refs[:2], refs[2:]
    rows = raw_ref.shape[0]
    rows_ref[...] = raw_ref[...]
    for half in range(2):

        @pl.when(pl.program_id(0) == half)
        def _():
            base_ref[...] = own_ref[...] + near_refs[half][rows:, :].astype(jnp.float32)


def gather_last_texts(raw, own, near):
    rows, width = raw.shape
    flat = pl.BlockSpec((rows // 4, width), lambda i: (2 * i + 1, 0))
    out = pl.BlockSpec((rows // 4, width), lambda i: (i, 0))
    return pl.pallas_call(
        gather_kernel,
        grid=(2,),
        out_shape=[like(rows // 2, width, raw.dtype), like(rows // 2, width, jnp.float32)],
        in_specs=[flat] * 2 + [IN_VMEM] * 2,
        out_specs=[out] * 2,
        compiler_params=params(14),
        cost_estimate=COST,
    )(raw, own, *near)


def last_texts_kernel(raw_ref, base_ref, *refs):
    last_refs, grad_ref = refs[:2], refs[-1]
    rows = grad_ref.shape[0]
    for half in range(2):

        @pl.when(pl.program_id(0) == half)
        def _():
            here = slice(half * rows, (half + 1) * rows)
            direction = base_ref[here, :] + last_refs[half][...].astype(jnp.float32)
            grad_ref[...] = finish_rows(raw_ref[here, :], direction)


def finish_last_texts(raw, base, last, held):
    rows, width = held.shape
    return pl.pallas_call(
        last_texts_kernel,
        grid=(2,),
        out_shape=like(rows, width, jnp.float32),
        in_specs=[IN_VMEM] * 4 + [pl.BlockSpec(memory_space=pl.ANY)],
        out_specs=pl.BlockSpec((rows // 4, width), lambda i: (2 * i + 1, 0)),
        input_output_aliases={4: 0},
        compiler_params=params(14),
        cost_estimate=COST,
    )(raw, base, *last, held)


def body(images_raw, texts_raw, inverse_softness, additive_shift_term):
    count = lax.axis_size("wide") * lax.axis_size("narrow")
    z = lax.axis_index("narrow") % RING
    scalars = jnp.concatenate([inverse_softness, additive_shift_term])
    slot = [jnp.where(z < RING - t, 1, 0).astype(jnp.int32).reshape(1) for t in range(RING)]
    slots = lambda *places: jnp.concatenate([slot[t] for t in places])
    up, down = ring_route(1, count), ring_route(-1, count)

    images_next_raw = send(images_raw, line_route(-RING, count))
    own_a, own_b = halves(texts_raw)
    left_a = send(own_a, up)
    right_b = send(own_b, down)
    images, text_own, own_sum = own_pair(scalars, texts_raw, images_raw)
    left_b = send(after(own_b, own_sum), up)
    right_a = send(after(own_a, own_sum), down)
    far_a = send(left_a, up)
    far_b = send(right_b, down)

    near_slots = slots(3, 1)
    left_part_a, right_part_b, images_next, weights, low = near_pairs(
        near_slots, scalars, images, images_next_raw, [left_a, right_b]
    )
    from_right_a = send(left_part_a, down)
    from_left_b = send(right_part_b, up)
    right_a1, right_a2, left_b1, left_b2, sums = pair_sums(
        near_slots, scalars, images, images_next, own_sum, weights, low, [right_a, left_b]
    )
    *far_parts, own_sum, next_sum = far_pair(
        slots(2), scalars, images, images_next, sums, [far_a, far_b]
    )
    far_a1, far_b1 = send(far_parts[0], up), send(far_parts[2], down)
    images_back = send(next_sum, line_route(RING, count))
    near = (from_right_a, from_left_b)
    far_a2 = send(after(far_parts[1], next_sum, *near), up)
    far_b2 = send(after(far_parts[3], next_sum, *near), down)

    rows_last, base_last = gather_last_texts(texts_raw, text_own, near)

    def relay(part, far, route):
        total = after(part, own_sum, base_last).astype(jnp.float32) + far.astype(jnp.float32)
        return send(total.astype(jnp.bfloat16), route)

    from_left_a1 = relay(right_a1, far_a1, up)
    from_right_b1 = relay(left_b1, far_b1, down)
    from_left_a2 = relay(right_a2, far_a2, up)
    from_right_b2 = relay(left_b2, far_b2, down)
    image_grad = finish_images(images_raw, own_sum, images_back)
    text_grad = finish_first_texts(texts_raw, text_own, near, (from_left_a1, from_right_b1))
    text_grad = finish_last_texts(
        rows_last, after(base_last, image_grad), (from_left_a2, from_right_b2), text_grad
    )
    return image_grad, text_grad


def solution(mesh):
    spec = P(AXES, None)
    return jax.shard_map(
        body,
        mesh=mesh,
        in_specs=(spec, spec, P(), P()),
        out_specs=(spec, spec),
        check_vma=False,
    )
```
